256 devices in a mesh: row: 8 (over x, core), col: 8 (over z_hi, y), depth: 4 (over z_lo).
Axes of the slice: x: 4, y: 4, z: 8 (z_hi: 2, z_lo: 4; z = z_hi * 4 + z_lo), core: 2. Of those that a mesh axis runs over, the one named last changes fastest.
Arguments:
- amplitudes: bfloat16 [6400, 60000], P('row', ('col', 'depth')), may hold values from -6 to 6
- integrals: bfloat16 [60000, 2400], P(('col', 'depth'), 'row'), may hold values from -0.125 to 0.125
- virtual_irrep: int32 [600], replicated, may hold values from 0 to 7
- occupied_irrep: int32 [100], replicated, may hold values from 0 to 7
- row_start: int32 [1], replicated, may hold values from 0 to 536
- column_start: int32 [1], replicated, may hold values from 0 to 576
Outputs:
- cycle: bfloat16 [2400, 6400], P(('col', 'depth'), 'row')
The draws below stay inside these ranges and needn't reach their ends.
All inputs are finite; a program needn't handle non-finite values.
Results may differ from the reference program's by a relative error of at most 0.001.
Values may be sent and summed in bfloat16 or wider, within the bound.
No kernel may reach another device: no remote copies, remote signals or barrier semaphores. Data moves between devices by JAX's collectives and lax.ppermute only.
A program may use at most 64 MiB of HBM per device.

```python
import jax
import jax.numpy as jnp
from jax import lax

O = 100
V = 600
VA = 64
VB = 24
ROWS = 6400
COLS = 2400
PAIRS = 60000


def set_ends(array, key, low, top_value):
    place = [jax.random.randint(jax.random.fold_in(key, axis), (), 0, length) for axis, length in enumerate(array.shape)]
    widest = array.shape.index(max(array.shape))
    beside = place[:widest] + [(place[widest] + 1) % array.shape[widest]] + place[widest + 1:]
    return array.at[tuple(place)].set(low).at[tuple(beside)].set(top_value)


def with_spikes(array, own_key, source, target, blocks, factor):
    owner, partner = [(jnp.arange(array.shape[dim]) // (array.shape[dim] // blocks)).reshape([-1 if axis == dim else 1 for axis in range(array.ndim)]) for dim in (source, target)]
    chosen = jax.random.permutation(own_key, blocks)[partner]
    strong = (owner == chosen) | (owner == (partner + blocks // 2) % blocks)
    return jnp.where(strong, factor * array, array)


def steps_of(own_key, extent, shards, low, top_value):
    def one(axis_at, shards_of):
        draws = jax.random.uniform(jax.random.fold_in(jax.random.fold_in(own_key, 6), axis_at), (shards_of,), jnp.float32, low / len(shards), top_value / len(shards))
        return jnp.repeat(jnp.exp(draws), extent[axis_at] // shards_of).reshape((-1,) + (1,) * (len(extent) - axis_at - 1))

    loudness = one(*shards[0])
    for cut in shards[1:]:
        loudness = loudness * one(*cut)
    return loudness


def centred(stream_key, shape, deviation, most, pieces=(), kind=jnp.bfloat16):
    result = jax.random.normal(stream_key, shape, jnp.float32) * deviation
    if len(pieces) > 0:
        result = steps_of(stream_key, shape, pieces, -0.22, 0.18) * result
    return jnp.clip(result, min=-most, max=most).astype(kind)


def heavy_noise(stream_key, dims, deviation, reach, split, heavy, kind=jnp.bfloat16):
    entries = deviation * jax.random.normal(stream_key, dims, jnp.float32)
    if split:
        entries = entries * steps_of(stream_key, dims, split, -0.22, 0.18)
    return jnp.clip(with_spikes(entries, jax.random.fold_in(stream_key, 3), *heavy), -reach, reach).astype(kind)


def setup_inputs(seed: int = 0) -> dict:
    seeds = jax.random.split(jax.random.key(seed), 7)
    amplitudes = centred(seeds[0], (ROWS, PAIRS), 1.0, 6.0, ((0, 8), (1, 32)))
    integrals = heavy_noise(seeds[1], (PAIRS, COLS), (V * O // 8) ** -0.5, 0.125, ((0, 32), (1, 8)), (0, 1, 32, 2.75))
    virtual_irrep = set_ends(jax.random.randint(seeds[2], (V,), 0, 8), jax.random.fold_in(seeds[2], 1), 0, 7).astype(jnp.int32)
    occupied_irrep = set_ends(jax.random.randint(seeds[3], (O,), 0, 8), jax.random.fold_in(seeds[3], 1), 0, 7).astype(jnp.int32)
    row_start = jax.random.randint(seeds[4], (1,), 0, V - VA + 1).astype(jnp.int32)
    column_start = jax.random.randint(seeds[5], (1,), 0, V - VB + 1).astype(jnp.int32)
    return dict(amplitudes=amplitudes, integrals=integrals, virtual_irrep=virtual_irrep, occupied_irrep=occupied_irrep, row_start=row_start, column_start=column_start)


def pair_labels(virtual_part, occupied_irrep):
    return jnp.bitwise_xor(virtual_part[:, None], occupied_irrep[None, :]).reshape(-1)


def reference(amplitudes, integrals, virtual_irrep, occupied_irrep, row_start, column_start):
    row_virtual = lax.dynamic_slice_in_dim(virtual_irrep, row_start[0].astype(jnp.int32), VA)
    column_virtual = lax.dynamic_slice_in_dim(virtual_irrep, column_start[0].astype(jnp.int32), VB)
    row_label = pair_labels(row_virtual, occupied_irrep)
    column_label = pair_labels(column_virtual, occupied_irrep)
    pair_label = pair_labels(virtual_irrep, occupied_irrep)
    masked_amplitudes = jnp.where(row_label[:, None] == pair_label[None, :], amplitudes, jnp.zeros_like(amplitudes))
    masked_integrals = jnp.where(pair_label[:, None] == column_label[None, :], integrals, jnp.zeros_like(integrals))
    cycle = lax.dot_general(masked_integrals, masked_amplitudes, (((0,), (1,)), ((), ())), preferred_element_type=jnp.float32)
    return cycle.astype(jnp.bfloat16)
```

```python
import functools

import jax
import jax.numpy as jnp
from jax import lax
from jax.experimental import pallas as pl
from jax.experimental.pallas import tpu as pltpu
from jax.sharding import PartitionSpec as P

O = 100
VA = 64
VB = 24
PAIRS = 1875
PAIRS_PAD = 1920
ROWS = 800
COLUMNS = 300
OUT = 75
OUT_PAD = 80
SLOTS = 127
SLOT_LANES = 128
PACK = 64
F32 = jnp.float32
BF16 = jnp.bfloat16
I32 = jnp.int32
STEPS = 256.0
VMEM_LIMIT = 40 * 1024 * 1024


def iota(shape, dim):
    return lax.broadcasted_iota(I32, shape, dim)


def tenth(t):
    return (t * 5243) >> 19


def table_row(values):
    lane = iota((1, 128), 1)
    row = jnp.zeros((1, 128), I32)
    for at, value in enumerate(values):
        row = jnp.where(lane == at, value, row)
    return row


def occupied_values(occupied):
    return [occupied[k] for k in range(O)]


def virtual_values(virtual, start, count):
    return [virtual[jnp.minimum(start + n, 599)] for n in range(count)]


def lane_labels(occupied_row, virtual_row, k, c):
    n = k.shape[1]
    table = jnp.concatenate([occupied_row, virtual_row], axis=1).astype(F32)
    lane = iota((16, 256), 1)
    sub = iota((16, 256), 0)
    keep = ((sub == 0) & (lane < 128)) | ((sub == 1) & (lane >= 128))
    left = jnp.where(keep, jnp.broadcast_to(table, (16, 256)), 0.0).astype(BF16)
    place = iota((128, n), 0)
    right = jnp.concatenate(
        [jnp.where(place == k, 1.0, 0.0), jnp.where(place == c, 1.0, 0.0)], axis=0
    ).astype(BF16)
    both = jnp.dot(left, right, preferred_element_type=F32).astype(I32)
    return both[0:1] ^ both[1:2]


def column_labels(occupied_row, virtual_row, k, c):
    n = k.shape[0]
    lane = iota((n, 128), 1)
    left = jnp.concatenate(
        [jnp.where(lane == k, 1.0, 0.0), jnp.where(lane == c, 1.0, 0.0)], axis=1
    ).astype(BF16)
    occupied_column = jnp.transpose(jnp.broadcast_to(occupied_row, (128, 128)).astype(F32))
    virtual_column = jnp.transpose(jnp.broadcast_to(virtual_row, (128, 128)).astype(F32))
    zero = jnp.zeros((128, 128), F32)
    right = jnp.concatenate(
        [
            jnp.concatenate([occupied_column, zero], axis=1),
            jnp.concatenate([zero, virtual_column], axis=1),
        ],
        axis=0,
    ).astype(BF16)
    both = jnp.dot(left, right, preferred_element_type=F32).astype(I32)
    return both[:, :128] ^ both[:, 128:]


def pair_places(pair_block):
    base = pair_block * PAIRS
    first = lax.div(base, O)
    t = iota((1, PAIRS_PAD), 1) + (base - first * O)
    c = tenth(t)
    return first, t - c * O, c


def lane_rank(label):
    n = label.shape[1]
    same = iota((16, n), 0) == label
    earlier = jnp.where(iota((n, n), 0) < iota((n, n), 1), 1.0, 0.0).astype(BF16)
    counts = jnp.dot(jnp.where(same, 1.0, 0.0).astype(BF16), earlier, preferred_element_type=F32)
    return jnp.sum(jnp.where(same, counts, 0.0), axis=0, keepdims=True).astype(I32)


def pack_columns_kernel(virtual, occupied, starts, integrals, packed):
    row_block, pair_block, column_start, wpass = starts[0], starts[1], starts[3], starts[5]
    occupied_row = table_row(occupied_values(occupied))
    first, k_pair, c_pair = pair_places(pair_block)
    virtual_row = table_row(
        virtual_values(virtual, first, 20)
        + virtual_values(virtual, column_start + row_block * (COLUMNS // O), COLUMNS // O)
    )
    t = iota((1, 384), 1)
    c = tenth(t)
    label = lane_labels(
        occupied_row,
        virtual_row,
        jnp.concatenate([k_pair, t - c * O], axis=1),
        jnp.concatenate([c_pair, c + 20], axis=1),
    )
    label_pair = label[:, :PAIRS_PAD]
    label_column = jnp.where(t < COLUMNS, label[:, PAIRS_PAD:], -1)
    rank = lane_rank(label_column) - wpass * PACK
    key = jnp.where((rank >= 0) & (rank < PACK) & (t < COLUMNS), label_column * PACK + rank, -1)
    chosen = jnp.where(iota((8 * PACK, 384), 0) == key, 1.0, 0.0).astype(BF16)[:, :COLUMNS]
    moved = lax.dot_general(
        chosen, integrals[...], (((1,), (1,)), ((), ())), preferred_element_type=F32
    )
    total = jnp.zeros((PACK, PAIRS), F32)
    here = label_pair[:, :PAIRS]
    for g in range(8):
        total = jnp.where(here == g, moved[g * PACK : (g + 1) * PACK], total)
    packed[...] = jnp.zeros((PACK, PAIRS_PAD), BF16)
    packed[:, :PAIRS] = total.astype(BF16)


def pack_rows_kernel(
    virtual, occupied, starts, amplitudes, rows_packed, unpack, column_label, pair_label, row_places, staged
):
    row_block, pair_block, row_start, column_start = starts[0], starts[1], starts[2], starts[3]
    spass, wpass = starts[4], starts[5]
    occupied_row = table_row(occupied_values(occupied))
    first, k_pair, c_pair = pair_places(pair_block)
    virtual_row = table_row(
        virtual_values(virtual, first, 20)
        + virtual_values(virtual, row_start + row_block * (ROWS // O), ROWS // O)
    )
    t = iota((1, 896), 1)
    c = tenth(t)
    label = lane_labels(
        occupied_row,
        virtual_row,
        jnp.concatenate([k_pair, t - c * O], axis=1),
        jnp.concatenate([c_pair, c + 20], axis=1),
    )
    label_pair = label[:, :PAIRS_PAD]
    label_row = jnp.where(t < ROWS, label[:, PAIRS_PAD:], -1)
    rank = lane_rank(label_row) - spass * SLOTS
    taken = (rank >= 0) & (rank < SLOTS) & (t < ROWS)
    slot = jnp.where(taken, rank, -1)
    row_places[...] = jnp.where(
        iota((8, 896), 0) == 0, slot, jnp.where(iota((8, 896), 0) == 1, label_row, 0)
    )
    pair_bf16 = jnp.broadcast_to(label_pair, (16, PAIRS_PAD)).astype(F32).astype(BF16)
    pair_label[...] = pair_bf16

    p = iota((ROWS, 128), 0)
    a = tenth(p)
    row_column = column_labels(occupied_row, virtual_row, p - a * O, a + 20)
    row_column = row_column.astype(F32).astype(BF16)
    wide = jnp.concatenate([row_column] * (PAIRS_PAD // 128), axis=1)[:, :PAIRS]
    masked = jnp.where(wide == pair_bf16[0:1, :PAIRS], amplitudes[...], jnp.zeros((), BF16))
    chosen = jnp.where(iota((SLOT_LANES, 896), 0) == slot, 1.0, 0.0).astype(BF16)[:, :ROWS]
    staged[...] = jnp.zeros((SLOT_LANES, PAIRS_PAD), F32)
    staged[:, :PAIRS] = jnp.dot(chosen, masked, preferred_element_type=F32)
    rows_packed[...] = jnp.transpose(staged[...]).astype(BF16)

    window = table_row(virtual_values(virtual, column_start, VB))
    x, core = lax.div(row_block, 2), lax.rem(row_block, 2)
    e = iota((OUT_PAD, 128), 0)
    lane = iota((4 * OUT_PAD, 128), 1)
    earlier = jnp.where(
        iota((4 * OUT_PAD, 4 * OUT_PAD), 1) < iota((4 * OUT_PAD, 4 * OUT_PAD), 0), 1.0, 0.0
    ).astype(BF16)
    for step in range(4):
        for half in range(2):
            shard = lax.rem(x - step + 4, 4) * 2 + half
            t = jnp.concatenate([e + d * OUT for d in range(4)], axis=0)
            valid = jnp.concatenate([e] * 4, axis=0) < OUT
            b = tenth(t)
            labels = column_labels(occupied_row, window, t - b * O, b + shard * (COLUMNS // O))
            labels = jnp.where(valid, labels, -1)
            same = labels == lane
            counts = jnp.dot(earlier, jnp.where(same, 1.0, 0.0).astype(BF16), preferred_element_type=F32)
            rank = jnp.sum(jnp.where(same, counts, 0.0), axis=1, keepdims=True).astype(I32) - wpass * PACK
            at = jnp.where((rank >= 0) & (rank < PACK), rank + PACK * jnp.bitwise_xor(core, half), -1)
            mine = jnp.where(valid & (lane == at), 1.0, 0.0).astype(BF16)
            rows = pl.ds((step * 2 + half) * 4 * OUT_PAD, 4 * OUT_PAD)
            unpack[rows, :] = mine
            column_label[rows, :] = labels.astype(F32).astype(BF16)


def contract_kernel(starts, unpack, column_label, pair_label, rows_packed, *refs):
    shards, sums = refs[:8], refs[8]
    x = lax.div(starts[0], 2)
    rows = rows_packed[...]
    here = pair_label[...][0:1]
    n = 4 * OUT_PAD
    lane = iota((n, SLOT_LANES), 1)
    for step in range(4):
        pair = jnp.concatenate([shards[2 * step][...], shards[2 * step + 1][...]], axis=0)
        for half in range(2):
            at = pl.ds((step * 2 + half) * n, n)
            spread = jnp.dot(unpack[at, :], pair, preferred_element_type=F32).astype(BF16)
            wide = jnp.concatenate([column_label[at, :]] * (PAIRS_PAD // 128), axis=1)
            masked = jnp.where(wide == here, spread, jnp.zeros((), BF16))
            part = jnp.dot(masked, rows, preferred_element_type=F32)
            top = jnp.max(jnp.abs(part), axis=1, keepdims=True)
            exponent = jnp.ceil(jnp.log2(jnp.maximum(top, 2.0**-120)) * STEPS)
            back = jnp.exp2(15.0 - exponent * (1.0 / STEPS))
            coded = jnp.clip(jnp.round(part * back), -32767.0, 32767.0)
            coded = jnp.where(lane == SLOTS, exponent, coded).astype(I32).astype(jnp.int16)
            shard = lax.rem(x - step + 4, 4) * 2 + half
            for d in range(4):
                sums[shard * 4 + d] = coded[d * OUT_PAD : (d + 1) * OUT_PAD]


def spread_kernel(virtual, occupied, starts, row_places, parts, out):
    column_start, place = starts[3], starts[6]
    occupied_row = table_row(occupied_values(occupied))
    first = lax.div(place * OUT, O)
    virtual_row = table_row(virtual_values(virtual, column_start + first, 2))
    t = iota((OUT_PAD, 128), 0) + (place * OUT - first * O)
    c = tenth(t)
    labels = column_labels(occupied_row, virtual_row, t - c * O, c)
    labels = labels.astype(F32)
    total = jnp.zeros((OUT_PAD, SLOT_LANES), F32)
    for d in range(parts.shape[0]):
        part = parts[d].astype(I32).astype(F32)
        total = total + part * jnp.exp2(part[:, SLOTS:] * (1.0 / STEPS) - 15.0)
    lane = iota((OUT_PAD, SLOT_LANES), 1)
    total = jnp.where(lane < SLOTS, total, 0.0).astype(BF16)
    slot = row_places[0:1, :]
    label_row = row_places[1:2, :].astype(F32)
    chosen = jnp.where(iota((SLOT_LANES, 896), 0) == slot, 1.0, 0.0).astype(BF16)
    spread = jnp.dot(total, chosen, preferred_element_type=F32)
    wide = jnp.concatenate([labels] * 7, axis=1)
    spread = jnp.where(wide == label_row, spread, 0.0).astype(BF16)
    out[...] = spread[:OUT, :ROWS]


SMEM = pl.BlockSpec(memory_space=pltpu.SMEM)
VMEM = pl.BlockSpec(memory_space=pltpu.VMEM)


def call(kernel, name, ins, outs, scratch=(), flops=0, moved=0):
    return pl.pallas_call(
        kernel,
        name=name,
        in_specs=ins,
        out_specs=[VMEM] * len(outs) if len(outs) > 1 else VMEM,
        out_shape=outs if len(outs) > 1 else outs[0],
        scratch_shapes=scratch,
        compiler_params=pltpu.CompilerParams(vmem_limit_bytes=VMEM_LIMIT),
        cost_estimate=pl.CostEstimate(flops=flops, bytes_accessed=moved, transcendentals=0),
    )


def shape(dims, kind):
    return jax.ShapeDtypeStruct(dims, kind)


def one_pass(amplitudes, integrals, virtual_irrep, occupied_irrep, starts):
    packed = call(
        pack_columns_kernel,
        "pack_columns",
        [SMEM, SMEM, SMEM, VMEM],
        [shape((PACK, PAIRS_PAD), BF16)],
        flops=2 * 8 * PACK * COLUMNS * PAIRS,
        moved=2 * PAIRS * (COLUMNS + PACK),
    )(virtual_irrep, occupied_irrep, starts, integrals)
    sibling = [(i, i ^ 1) for i in range(8)]
    own = [packed]
    for step in range(1, 4):
        own.append(lax.ppermute(packed, "row", [(i, (i + 2 * step) % 8) for i in range(8)]))
    other = [lax.ppermute(block, "row", sibling) for block in own]
    shards = [block for pair in zip(own, other) for block in pair]
    rows_packed, unpack, column_label, pair_label, row_places = call(
        pack_rows_kernel,
        "pack_rows",
        [SMEM, SMEM, SMEM, VMEM],
        [
            shape((PAIRS_PAD, SLOT_LANES), BF16),
            shape((8 * 4 * OUT_PAD, 128), BF16),
            shape((8 * 4 * OUT_PAD, 128), BF16),
            shape((16, PAIRS_PAD), BF16),
            shape((8, 896), I32),
        ],
        [pltpu.VMEM((SLOT_LANES, PAIRS_PAD), F32)],
        flops=8 * 2 * SLOT_LANES * ROWS * PAIRS,
        moved=2 * PAIRS * ROWS * 3,
    )(virtual_irrep, occupied_irrep, starts, amplitudes)
    sums = call(
        contract_kernel,
        "contract",
        [SMEM] + [VMEM] * 12,
        [shape((32, OUT_PAD, SLOT_LANES), jnp.int16)],
        flops=2 * 2400 * PAIRS_PAD * 256,
        moved=2 * 8 * PACK * PAIRS_PAD,
    )(starts, unpack, column_label, pair_label, rows_packed, *shards)
    parts = lax.all_to_all(sums, ("col", "depth"), 0, 0)
    return call(
        spread_kernel,
        "spread",
        [SMEM, SMEM, SMEM, VMEM, VMEM],
        [shape((OUT, ROWS), BF16)],
        flops=2 * OUT * ROWS * 128,
        moved=2 * 32 * OUT_PAD * SLOT_LANES,
    )(virtual_irrep, occupied_irrep, starts, row_places, parts)


def most(labels):
    return jnp.max(jnp.sum((labels[:, None, :] == jnp.arange(8)[None, :, None]).astype(I32), axis=2))


def body(amplitudes, integrals, virtual_irrep, occupied_irrep, row_start, column_start):
    row_block = lax.axis_index("row").astype(I32)
    pair_block = lax.axis_index(("col", "depth")).astype(I32)

    def starts(spass, wpass):
        return jnp.stack(
            [
                row_block,
                pair_block,
                row_start[0],
                column_start[0],
                jnp.asarray(spass, I32),
                jnp.asarray(wpass, I32),
                pair_block,
                jnp.zeros((), I32),
            ]
        )

    run = functools.partial(one_pass, amplitudes, integrals, virtual_irrep, occupied_irrep)
    first = run(starts(0, 0))

    def labels_of(start, count, blocks):
        part = lax.dynamic_slice_in_dim(virtual_irrep, start[0], count)
        return jnp.bitwise_xor(
            part.reshape(blocks, count // blocks, 1), occupied_irrep[None, None, :]
        ).reshape(blocks, -1)

    spasses = lax.div(most(labels_of(row_start, VA, 8)) + (SLOTS - 1), SLOTS)
    wpasses = lax.div(most(labels_of(column_start, VB, 8)) + (PACK - 1), PACK)
    passes = spasses * wpasses

    def more(state):
        return state[0] < passes

    def again(state):
        at, out = state
        wpass = lax.rem(at, wpasses)
        return at + 1, out + run(starts(lax.div(at, wpasses), wpass))

    return lax.while_loop(more, again, (jnp.ones((), I32), first))[1]


def solution(mesh):
    return jax.shard_map(
        body,
        mesh=mesh,
        in_specs=(P("row", ("col", "depth")), P(("col", "depth"), "row"), P(), P(), P(), P()),
        out_specs=P(("col", "depth"), "row"),
        check_vma=False,
    )
```

```python
import functools

import jax
import jax.numpy as jnp
from jax import lax
from jax.experimental import pallas as pl
from jax.experimental.pallas import tpu as pltpu
from jax.sharding import PartitionSpec as P

O = 100
VA = 64
VB = 24
PAIRS = 1875
PAIRS_PAD = 1920
ROWS = 800
COLUMNS = 300
OUT = 75
OUT_PAD = 80
SLOTS = 127
SLOT_LANES = 128
MORE = 15
MORE_ROWS = (OUT_PAD - OUT) * 8
PACK = 64
F32 = jnp.float32
BF16 = jnp.bfloat16
I32 = jnp.int32
STEPS = 256.0
VMEM_LIMIT = 40 * 1024 * 1024


def iota(shape, dim):
    return lax.broadcasted_iota(I32, shape, dim)


def tenth(t):
    return (t * 5243) >> 19


def table_row(values):
    lane = iota((1, 128), 1)
    row = jnp.zeros((1, 128), I32)
    for at, value in enumerate(values):
        row = jnp.where(lane == at, value, row)
    return row


def occupied_values(occupied):
    return [occupied[k] for k in range(O)]


def virtual_values(virtual, start, count):
    return [virtual[jnp.minimum(start + n, 599)] for n in range(count)]


def one_hot(flags):
    return jnp.where(flags, 1.0, 0.0).astype(BF16)


def from_tables(occupied_rows, virtual_row, k, c):
    n, count = k.shape[1], len(occupied_rows)
    sub = iota((16, 128), 0)
    left = jnp.zeros((16, 128), I32)
    for at, row in enumerate(occupied_rows):
        left = jnp.where(sub == at, row, left)
    right = jnp.where(sub[:, :32] == count, virtual_row[:, :32], 0)
    left = jnp.concatenate([left.astype(F32), right.astype(F32)], axis=1).astype(BF16)
    places = jnp.concatenate(
        [one_hot(iota((128, n), 0) == k), one_hot(iota((32, n), 0) == c)], axis=0
    )
    found = jnp.dot(left, places, preferred_element_type=F32).astype(I32)
    return [found[at : at + 1] for at in range(count + 1)]


def down_table(row, k):
    table = jnp.broadcast_to(row.astype(F32), (128, 128)).astype(BF16)
    places = one_hot(iota(k.shape, 1) == k)
    found = lax.dot_general(
        places, table, (((1,), (1,)), ((), ())), preferred_element_type=F32
    )
    return found.astype(I32)


def pick(values, at):
    result = jnp.full(at.shape, values[0], I32)
    for n, value in enumerate(values[1:], 1):
        result = jnp.where(at == n, value, result)
    return result


def pair_places(pair_block):
    base = pair_block * PAIRS
    first = lax.div(base, O)
    t = iota((1, PAIRS_PAD), 1) + (base - first * O)
    c = tenth(t)
    return first, t - c * O, c


def lane_rank(label):
    n = label.shape[1]
    same = iota((16, n), 0) == label
    earlier = one_hot(iota((n, n), 0) < iota((n, n), 1))
    counts = jnp.dot(one_hot(same), earlier, preferred_element_type=F32)
    return jnp.sum(jnp.where(same, counts, 0.0), axis=0, keepdims=True).astype(I32)


def label_counts(occupied_row, value, labels):
    same = ((occupied_row ^ value) == labels) & (iota(labels.shape, 1) < O)
    return jnp.sum(jnp.where(same, 1.0, 0.0), axis=1, keepdims=True)


def places():
    row_block = lax.axis_index("row").astype(I32)
    pair_block = (lax.axis_index("col") * 4 + lax.axis_index("depth")).astype(I32)
    return row_block, pair_block


def start_copies(arrived, *pairs):
    copies = []
    for at, (source, target) in enumerate(pairs):
        copies.append(pltpu.make_async_copy(source, target, arrived.at[at]))
        copies[-1].start()
    return copies


def pack_columns_kernel(
    virtual_hbm,
    occupied_hbm,
    column_start_hbm,
    turn_hbm,
    integrals_hbm,
    packed,
    pair_label,
    table,
    integrals,
    virtual,
    occupied,
    column_start,
    turn,
    arrived,
):
    fetch = start_copies(
        arrived,
        (occupied_hbm, occupied),
        (virtual_hbm, virtual),
        (column_start_hbm, column_start),
        (turn_hbm, turn),
        (integrals_hbm, integrals),
    )
    row_block, pair_block = places()
    packed[...] = jnp.zeros((PACK, PAIRS_PAD), BF16)
    first, k_pair, c_pair = pair_places(pair_block)
    fetch[0].wait()
    occupied_row = table_row(occupied_values(occupied))
    for copy in fetch[1:4]:
        copy.wait()
    wpass = turn[1]
    blocks = COLUMNS // O
    own = virtual_values(virtual, column_start[0] + row_block * blocks, blocks)
    virtual_row = table_row(virtual_values(virtual, first, 20) + own)
    t = iota((1, 384), 1)
    c = tenth(t)
    found = from_tables(
        [occupied_row],
        virtual_row,
        jnp.concatenate([k_pair, t - c * O], axis=1),
        jnp.concatenate([c_pair, c + 20], axis=1),
    )
    label = found[0] ^ found[1]
    here = label[:, :PAIRS_PAD].astype(F32).astype(BF16)
    pair_label[...] = jnp.broadcast_to(here, (16, PAIRS_PAD))
    table[...] = jnp.broadcast_to(occupied_row, (8, 128))
    rank = lane_rank(jnp.where(t < COLUMNS, label[:, PAIRS_PAD:], -1)) - wpass * PACK
    chosen = one_hot((iota((PACK, 384), 0) == rank) & (t < COLUMNS))[:, :COLUMNS]
    r = iota((COLUMNS, 128), 0)
    b = tenth(r)
    column = down_table(occupied_row, r - b * O) ^ pick(own, b)
    column = column.astype(F32).astype(BF16)
    wide = jnp.concatenate([column] * (PAIRS_PAD // 128), axis=1)[:, :PAIRS]
    fetch[4].wait()
    masked = jnp.where(wide == here[:, :PAIRS], integrals[...], jnp.zeros((), BF16))
    packed[:, :PAIRS] = jnp.dot(chosen, masked, preferred_element_type=F32).astype(BF16)


def fullest(occupied_row, window, count, size):
    sub, lane = iota((16, 128), 0), iota((16, 128), 1)
    at, block = iota((128, 128), 0), iota((128, 128), 1)
    blocks = one_hot((at >= block * size) & (at < (block + 1) * size))
    virtuals = jnp.dot(one_hot((window == sub) & (lane < count)), blocks, preferred_element_type=F32)
    total = jnp.zeros((16, 128), F32)
    for h in range(8):
        total = total + label_counts(occupied_row, h, sub) * virtuals[h : h + 1]
    return total


def places_past(labels, lane, more_labels, earlier):
    past = jnp.dot(one_hot(labels == lane), more_labels, preferred_element_type=F32)
    before = jnp.dot(earlier, past.astype(BF16), preferred_element_type=F32)
    return jnp.where(past > 0.5, before, -1.0)


def pack_rows_kernel(
    virtual_hbm,
    row_start_hbm,
    column_start_hbm,
    turn_hbm,
    pair_label,
    table,
    amplitudes_hbm,
    rows_packed,
    unpack,
    column_label,
    row_places,
    more,
    more_labels,
    rows_more,
    column_more,
    left_over,
    spasses,
    wpasses,
    staged,
    amplitudes,
    virtual,
    row_start,
    column_start,
    turn,
    arrived,
):
    fetch = start_copies(
        arrived,
        (virtual_hbm, virtual),
        (row_start_hbm, row_start),
        (column_start_hbm, column_start),
        (turn_hbm, turn),
        (amplitudes_hbm, amplitudes),
    )
    row_block, _ = places()
    occupied_row = table[0:1]
    occupied_rank = lane_rank(jnp.where(iota((1, 128), 1) < O, occupied_row, -1))
    sub = iota((16, 128), 0)
    e = iota((OUT_PAD, 128), 0)
    t = jnp.concatenate([e + d * OUT for d in range(4)], axis=0)
    valid = jnp.concatenate([e] * 4, axis=0) < OUT
    b = tenth(t)
    occupied_here = down_table(occupied_row, t - b * O)
    rank_here = down_table(occupied_rank, t - b * O)
    p = iota((ROWS, 128), 0)
    p_block = tenth(p)
    row_column = down_table(occupied_row, p - p_block * O)
    for copy in fetch[:4]:
        copy.wait()
    spass, wpass = turn[0], turn[1]
    rank_here = rank_here - wpass * PACK

    own = virtual_values(virtual, row_start[0] + row_block * (ROWS // O), ROWS // O)
    t = iota((1, 896), 1)
    a = tenth(t)
    found = from_tables([occupied_row, occupied_rank], table_row(own), t - a * O, a)
    label_row = jnp.where(t < ROWS, found[0] ^ found[2], -1)
    before = jnp.zeros((16, 896), F32)
    for n, value in enumerate(own):
        before = before + jnp.where(a > n, label_counts(occupied_row, value, sub), 0.0)
    before = jnp.where(iota((16, 896), 0) == label_row, before, 0.0)
    rank = found[1] + jnp.sum(before, axis=0, keepdims=True).astype(I32) - spass * SLOTS
    slot = jnp.where((rank >= 0) & (rank < SLOTS) & (t < ROWS), rank, -1)
    at = iota((8, 896), 0)
    row_places[...] = jnp.where(at == 0, slot, jnp.where(at == 1, label_row, jnp.where(t < ROWS, rank, -1)))

    columns = virtual_values(virtual, column_start[0], VB)
    window = table_row(columns)
    row_window = table_row(virtual_values(virtual, row_start[0], VA))
    row_counts = fullest(occupied_row, row_window, VA, 8)
    most = jnp.max(row_counts).astype(I32)
    column_counts = fullest(occupied_row, window, VB, 3)
    wpasses[0] = lax.div(jnp.max(column_counts).astype(I32) + (PACK - 1), PACK)
    spasses[0] = lax.div(most + (SLOTS - 1), SLOTS)
    more[...] = jnp.zeros((8, 128), F32)

    @pl.when((most > SLOTS) & (most <= SLOTS + MORE))
    def _():
        t = iota((1, 2432), 1)
        b = tenth(t)
        found = from_tables([occupied_row], window, t - b * O, b)
        same = (iota((16, 2432), 0) == (found[0] ^ found[1])) & (t < VB * O)
        at, block = iota((2432, 128), 0), iota((2432, 128), 1)
        blocks = one_hot((at >= block * OUT) & (at < (block + 1) * OUT))
        in_block = jnp.dot(one_hot(same), blocks, preferred_element_type=F32)
        past = row_counts > SLOTS
        found = lax.dot_general(
            one_hot(past), in_block.astype(BF16), (((0,), (0,)), ((), ())), preferred_element_type=F32
        )
        fits = jnp.max(found).astype(I32) <= MORE_ROWS
        spasses[0] = jnp.where(fits, 1, spasses[0])
        mine = past & (iota((16, 128), 1) == row_block)
        mine = jnp.sum(jnp.where(mine, 1.0, 0.0), axis=1, keepdims=True)
        mine = jnp.where(fits, jnp.broadcast_to(mine, (16, 128)), 0.0)
        more[...] = jnp.broadcast_to(jnp.max(mine), (8, 128))
        more_labels[...] = jnp.zeros((128, 128), BF16)
        more_labels[:16] = mine.astype(BF16)

    left_over[0] = spasses[0] * wpasses[0] - 1

    x, core = lax.div(row_block, 2), lax.rem(row_block, 2)
    lane = iota((4 * OUT_PAD, 128), 1)
    key = iota((128, 128), 0)
    key_label = key & 7
    key_block = key >> 3
    for step in range(4):
        for half in range(2):
            shard = lax.rem(x - step + 4, 4) * 2 + half
            blocks = [
                virtual[jnp.minimum(column_start[0] + shard * (COLUMNS // O) + n, 599)] for n in range(3)
            ]
            labels = jnp.where(valid, occupied_here ^ pick(blocks, b), -1)
            before = jnp.zeros((128, 1), F32)
            for n in range(2):
                before = before + jnp.where(
                    key_block[:, :1] > n, label_counts(occupied_row, blocks[n], key_label), 0.0
                )
            before = jnp.where(key_block < 3, jnp.broadcast_to(before, (128, 128)), 0.0)
            at = jnp.dot(
                one_hot((lane == b * 8 + labels) & valid), before.astype(BF16), preferred_element_type=F32
            ).astype(I32)
            at = at + rank_here
            at = jnp.where((at >= 0) & (at < PACK) & valid, at + PACK * jnp.bitwise_xor(core, half), -1)
            rows = pl.ds((step * 2 + half) * 4 * OUT_PAD, 4 * OUT_PAD)
            unpack[rows, :] = one_hot(lane == at)
            column_label[rows, :] = labels.astype(F32).astype(BF16)

    row_column = row_column ^ pick(own, p_block)
    wide = jnp.concatenate([row_column.astype(F32).astype(BF16)] * (PAIRS_PAD // 128), axis=1)
    chosen = one_hot(iota((SLOT_LANES, 896), 0) == slot)[:, :ROWS]
    here = pair_label[0:1, :PAIRS]
    fetch[4].wait()
    masked = jnp.where(wide[:, :PAIRS] == here, amplitudes[...], jnp.zeros((), BF16))
    staged[...] = jnp.zeros((SLOT_LANES, PAIRS_PAD), F32)
    staged[:, :PAIRS] = jnp.dot(chosen, masked, preferred_element_type=F32)
    rows_packed[...] = jnp.transpose(staged[...]).astype(BF16)

    @pl.when(jnp.max(more[...]) > 0.0)
    def _():
        sub = iota((SLOT_LANES, 896), 0) & 15
        past = row_places[2:3, :] - SLOTS
        chosen = one_hot((sub == past) & (sub < MORE))[:, :ROWS]
        wide = jnp.concatenate([row_column.astype(F32).astype(BF16)] * (PAIRS_PAD // 128), axis=1)
        masked = jnp.where(
            wide[:, :PAIRS] == pair_label[0:1, :PAIRS], amplitudes[...], jnp.zeros((), BF16)
        )
        staged[:, :PAIRS] = jnp.dot(chosen, masked, preferred_element_type=F32)
        rows_more[...] = jnp.transpose(staged[...]).astype(BF16)
        n = 4 * OUT_PAD
        lane = iota((n, 128), 1)
        row, column = iota((n, n), 0), iota((n, n), 1)
        earlier = (column < row) & (lax.div(column, OUT_PAD) == lax.div(row, OUT_PAD))
        for shard in range(8):
            rows = pl.ds(shard * n, n)
            labels = column_label[rows, :].astype(F32).astype(I32)
            column_more[rows, :] = places_past(labels, lane, more_labels[...], one_hot(earlier))


def contract_kernel(
    steps, unpack, column_label, pair_label, rows_packed, more, rows_more, column_more, *refs
):
    shards, (sums, coded_rows, held, sent) = refs[: 2 * len(steps)], refs[-4:]
    any_more = jnp.max(more[...]) > 0.0
    x = lax.div(places()[0], 2)
    rows = rows_packed[...]
    here = pair_label[0:1]
    n = 8 * OUT_PAD
    lane = iota((n, SLOT_LANES), 1)
    copies = []
    for place, step in enumerate(steps):
        at = pl.ds(step * n, n)

        def unpacked():
            pair = jnp.concatenate([shards[2 * place][...], shards[2 * place + 1][...]], axis=0)
            spread = jnp.dot(unpack[at, :], pair, preferred_element_type=F32).astype(BF16)
            wide = jnp.concatenate([column_label[at, :]] * (PAIRS_PAD // 128), axis=1)
            return jnp.where(wide == here, spread, jnp.zeros((), BF16))

        held[...] = jnp.dot(unpacked(), rows, preferred_element_type=F32)

        @pl.when(any_more)
        def _():
            past = jnp.dot(unpacked(), rows_more[...], preferred_element_type=F32)
            to = column_more[at, :].astype(I32)
            past = jnp.where((to >= 0) & ((to & 7) == (lane >> 4)), past, 0.0)
            target = lax.div(iota((n, 128), 0), OUT_PAD) * 8 + (8 - OUT_PAD + OUT) + (to >> 3)
            moved = lax.dot_general(
                jnp.where((to >= 0) & (lane == target), 1.0, 0.0),
                past,
                (((0,), (0,)), ((), ())),
                precision=lax.Precision.HIGHEST,
                preferred_element_type=F32,
            )
            for d in range(8):
                pad = pl.ds((d + 1) * OUT_PAD - 8, 8)
                held[pad, :] = held[pad, :] + moved[d * 8 : (d + 1) * 8]

        part = held[...]
        top = jnp.max(jnp.abs(part), axis=1, keepdims=True)
        exponent = jnp.ceil(jnp.log2(jnp.maximum(top, 2.0**-120)) * STEPS)
        back = jnp.exp2(15.0 - exponent * (1.0 / STEPS))
        coded = jnp.clip(jnp.round(part * back), -32767.0, 32767.0)
        coded = jnp.where(lane == SLOTS, exponent, coded).astype(I32).astype(jnp.int16)
        for d in range(8):
            coded_rows[place * 8 + d] = coded[d * OUT_PAD : (d + 1) * OUT_PAD]
        copy = pltpu.make_async_copy(
            coded_rows.at[pl.ds(place * 8, 8)],
            sums.at[pl.ds(lax.rem(x - step + 4, 4) * 8, 8)],
            sent.at[place],
        )
        copy.start()
        copies.append(copy)
    for copy in copies:
        copy.wait()


def place_kernel(
    virtual,
    occupied,
    column_start,
    row_places,
    more,
    more_labels,
    chosen,
    row_label,
    column_label,
    own_more,
):
    _, place = places()
    occupied_row = table_row(occupied_values(occupied))
    first = lax.div(place * OUT, O)
    t = iota((OUT_PAD, 128), 0) + (place * OUT - first * O)
    c = tenth(t)
    values = virtual_values(virtual, column_start[0] + first, 2)
    labels = down_table(occupied_row, t - c * O) ^ pick(values, c)
    column_label[...] = labels.astype(F32)

    @pl.when(jnp.max(more[...]) > 0.0)
    def _():
        row, column = iota((OUT_PAD, OUT_PAD), 0), iota((OUT_PAD, OUT_PAD), 1)
        e, lane = iota((OUT_PAD, 128), 0), iota((OUT_PAD, 128), 1)
        valid = jnp.where(e < OUT, labels, -1)
        own_more[...] = places_past(valid, lane, more_labels[...], one_hot(column < row))

    chosen[...] = one_hot(iota((SLOT_LANES, 896), 0) == row_places[0:1, :])
    row_label[...] = jnp.broadcast_to(row_places[1:2, :].astype(F32), (8, 896))


def spread_kernel(chosen, row_label, column_label, own_more, row_places, more, parts, others, out, held):
    total = jnp.zeros((OUT_PAD, SLOT_LANES), F32)
    for d in range(parts.shape[0]):
        part = parts[d].astype(I32).astype(F32)
        total = total + part * jnp.exp2(part[:, SLOTS:] * (1.0 / STEPS) - 15.0)
    lane = iota((OUT_PAD, SLOT_LANES), 1)
    total = jnp.where(lane < SLOTS, total, 0.0).astype(BF16)
    held[...] = jnp.dot(total, chosen[...], preferred_element_type=F32)

    @pl.when(jnp.max(more[...]) > 0.0)
    def _():
        to = own_more[...].astype(I32)
        source = one_hot((to >= 0) & (lane == OUT + (to >> 3)))[:, :OUT_PAD]
        past = jnp.dot(source, total, preferred_element_type=F32)
        past = jnp.where((to >= 0) & ((to & 7) == (lane >> 4)), past, 0.0).astype(BF16)
        sub = iota((SLOT_LANES, 896), 0) & 15
        moved = one_hot((sub == row_places[2:3, :] - SLOTS) & (sub < MORE))
        held[...] = held[...] + jnp.dot(past, moved, preferred_element_type=F32)

    wide = jnp.concatenate([column_label[...]] * 7, axis=1)
    spread = jnp.where(wide == row_label[0:1], held[...], 0.0).astype(BF16)
    out[...] = spread[:OUT, :ROWS] + others[...]


SMEM = pl.BlockSpec(memory_space=pltpu.SMEM)
VMEM = pl.BlockSpec(memory_space=pltpu.VMEM)
ANY = pl.BlockSpec(memory_space=pl.ANY)
HBM = pl.BlockSpec(memory_space=pltpu.HBM)


def call(kernel, name, ins, outs, scratch=(), flops=0, moved=0, out_specs=None, aliases=None):
    return pl.pallas_call(
        kernel,
        name=name,
        in_specs=ins,
        out_specs=out_specs or ([VMEM] * len(outs) if len(outs) > 1 else VMEM),
        out_shape=outs if len(outs) > 1 else outs[0],
        scratch_shapes=scratch,
        input_output_aliases=aliases or {},
        compiler_params=pltpu.CompilerParams(vmem_limit_bytes=VMEM_LIMIT),
        cost_estimate=pl.CostEstimate(flops=flops, bytes_accessed=moved, transcendentals=0),
    )


def shape(dims, kind):
    return jax.ShapeDtypeStruct(dims, kind)


def after(value, *others):
    return lax.optimization_barrier((value, *others))[0]


def one_pass(amplitudes, integrals, virtual, occupied, row_start, column_start, turn, others):
    packed, pair_label, table = call(
        pack_columns_kernel,
        "pack_columns",
        [HBM] * 5,
        [
            shape((PACK, PAIRS_PAD), BF16),
            shape((16, PAIRS_PAD), BF16),
            shape((8, 128), I32),
        ],
        [
            pltpu.VMEM((COLUMNS, PAIRS), BF16),
            pltpu.SMEM((600,), I32),
            pltpu.SMEM((O,), I32),
            pltpu.SMEM((1,), I32),
            pltpu.SMEM((2,), I32),
            pltpu.SemaphoreType.DMA((5,)),
        ],
        flops=2 * 8 * PACK * COLUMNS * PAIRS,
        moved=2 * PAIRS * (COLUMNS + PACK),
    )(virtual, occupied, column_start, turn, integrals.T)

    def along_x(step):
        return lax.ppermute(packed, "row", [(i, (i + 2 * step) % 8) for i in range(8)])

    def to_sibling(block):
        return lax.ppermute(block, "row", [(i, i ^ 1) for i in range(8)])

    from_1, from_3, from_2 = along_x(1), along_x(3), along_x(2)
    own_other = to_sibling(packed)
    (
        rows_packed,
        unpack,
        column_label,
        row_places,
        more,
        more_labels,
        rows_more,
        column_more,
        *passes,
    ) = call(
        pack_rows_kernel,
        "pack_rows",
        [HBM] * 4 + [VMEM] * 2 + [HBM],
        [
            shape((PAIRS_PAD, SLOT_LANES), BF16),
            shape((8 * 4 * OUT_PAD, 128), BF16),
            shape((8 * 4 * OUT_PAD, 128), BF16),
            shape((8, 896), I32),
            shape((8, 128), F32),
            shape((128, 128), BF16),
            shape((PAIRS_PAD, SLOT_LANES), BF16),
            shape((8 * 4 * OUT_PAD, 128), F32),
            shape((1,), I32),
            shape((1,), I32),
            shape((1,), I32),
        ],
        [
            pltpu.VMEM((SLOT_LANES, PAIRS_PAD), F32),
            pltpu.VMEM((ROWS, PAIRS), BF16),
            pltpu.SMEM((600,), I32),
            pltpu.SMEM((1,), I32),
            pltpu.SMEM((1,), I32),
            pltpu.SMEM((2,), I32),
            pltpu.SemaphoreType.DMA((5,)),
        ],
        flops=2 * SLOT_LANES * ROWS * PAIRS,
        moved=2 * PAIRS * ROWS * 3,
        out_specs=[VMEM] * 8 + [SMEM] * 3,
    )(virtual, row_start, column_start, turn, pair_label, table, amplitudes)

    def contract(steps, shards, sums):
        held = [] if sums is None else [sums]
        return call(
            functools.partial(contract_kernel, steps),
            "contract_" + "_".join(map(str, steps)),
            [VMEM] * (7 + len(shards)) + [ANY] * len(held),
            [shape((32, OUT_PAD, SLOT_LANES), jnp.int16)],
            [
                pltpu.VMEM((8 * len(steps), OUT_PAD, SLOT_LANES), jnp.int16),
                pltpu.VMEM((8 * OUT_PAD, SLOT_LANES), F32),
                pltpu.SemaphoreType.DMA((len(steps),)),
            ],
            flops=2 * 640 * len(steps) * PAIRS_PAD * 256,
            moved=2 * len(shards) * PACK * PAIRS_PAD,
            out_specs=ANY,
            aliases={} if sums is None else {7 + len(shards): 0},
        )(
            unpack,
            column_label,
            pair_label,
            rows_packed,
            more,
            rows_more,
            column_more,
            *shards,
            *held,
        )

    *found, own_more = call(
        place_kernel,
        "place",
        [SMEM] * 3 + [VMEM] * 3,
        [
            shape((SLOT_LANES, 896), BF16),
            shape((8, 896), F32),
            shape((OUT_PAD, 128), F32),
            shape((OUT_PAD, 128), F32),
        ],
    )(virtual, occupied, column_start, row_places, more, more_labels)
    from_1, from_3, rows_packed, *found = lax.optimization_barrier((from_1, from_3, rows_packed, *found))
    other_1, other_3 = to_sibling(from_1), to_sibling(from_3)
    sums = contract((0,), (packed, own_other), None)
    from_2, sums = lax.optimization_barrier((from_2, sums))
    other_2 = to_sibling(from_2)
    sums = contract((1, 3), (from_1, other_1, from_3, other_3), sums)
    sums = contract((2,), (from_2, other_2), sums)
    sums, *passes = lax.optimization_barrier((sums, *passes))
    parts = lax.all_to_all(sums, ("col", "depth"), 0, 0)
    return call(
        spread_kernel,
        "spread",
        [VMEM] * 8,
        [shape((OUT, ROWS), BF16)],
        [pltpu.VMEM((OUT_PAD, 896), F32)],
        flops=2 * OUT * ROWS * 128,
        moved=2 * 32 * OUT_PAD * SLOT_LANES,
    )(*found, own_more, row_places, more, parts, others(*passes))


def body(amplitudes, integrals, virtual_irrep, occupied_irrep, row_start, column_start):
    run = functools.partial(
        one_pass, amplitudes, integrals, virtual_irrep, occupied_irrep, row_start, column_start
    )
    def more(state):
        return state[0][0] > 0

    def again(state):
        left, out, spasses, wpasses = state
        turn = jnp.concatenate([lax.div(left, wpasses), lax.rem(left, wpasses)])
        return left - 1, run(turn, lambda *_: out), spasses, wpasses

    def other_passes(left, spasses, wpasses):
        nothing = jnp.zeros((OUT, ROWS), BF16)
        return lax.while_loop(more, again, (left, nothing, spasses, wpasses))[1]

    return run(jnp.zeros((2,), I32), other_passes)


def solution(mesh):
    return jax.shard_map(
        body,
        mesh=mesh,
        in_specs=(P("row", ("col", "depth")), P(("col", "depth"), "row"), P(), P(), P(), P()),
        out_specs=P(("col", "depth"), "row"),
        check_vma=False,
    )
```

```python
import functools

import jax
import jax.numpy as jnp
from jax import lax
from jax.experimental import pallas as pl
from jax.experimental.pallas import tpu as pltpu
from jax.sharding import PartitionSpec as P

O = 100
VA = 64
VB = 24
PAIRS = 1875
PAIRS_PAD = 1920
ROWS = 800
COLUMNS = 300
OUT = 75
OUT_PAD = 80
SLOTS = 127
SLOT_LANES = 128
MORE = 15
MORE_ROWS = (OUT_PAD - OUT) * 8
PACK = 64
F32 = jnp.float32
BF16 = jnp.bfloat16
I32 = jnp.int32
STEPS = 256.0
VMEM_LIMIT = 40 * 1024 * 1024


def iota(shape, dim):
    return lax.broadcasted_iota(I32, shape, dim)


def tenth(t):
    return (t * 5243) >> 19


def table_row(values):
    lane = iota((1, 128), 1)
    row = jnp.zeros((1, 128), I32)
    for at, value in enumerate(values):
        row = jnp.where(lane == at, value, row)
    return row


def occupied_values(occupied):
    return [occupied[k] for k in range(O)]


def virtual_values(virtual, start, count):
    return [virtual[jnp.minimum(start + n, 599)] for n in range(count)]


def one_hot(flags):
    return jnp.where(flags, 1.0, 0.0).astype(BF16)


def table_places(k, c):
    n = k.shape[1]
    return jnp.concatenate(
        [one_hot(iota((128, n), 0) == k), one_hot(iota((32, n), 0) == c)], axis=0
    )


def from_tables(occupied_rows, virtual_row, places):
    count = len(occupied_rows)
    sub = iota((16, 128), 0)
    left = jnp.zeros((16, 128), I32)
    for at, row in enumerate(occupied_rows):
        left = jnp.where(sub == at, row, left)
    right = jnp.where(sub[:, :32] == count, virtual_row[:, :32], 0)
    left = jnp.concatenate([left.astype(F32), right.astype(F32)], axis=1).astype(BF16)
    found = jnp.dot(left, places, preferred_element_type=F32).astype(I32)
    return [found[at : at + 1] for at in range(count + 1)]


def down_table(row, k):
    table = jnp.broadcast_to(row.astype(F32), (128, 128)).astype(BF16)
    places = one_hot(iota(k.shape, 1) == k)
    found = lax.dot_general(
        places, table, (((1,), (1,)), ((), ())), preferred_element_type=F32
    )
    return found.astype(I32)


def pick(values, at):
    result = jnp.full(at.shape, values[0], I32)
    for n, value in enumerate(values[1:], 1):
        result = jnp.where(at == n, value, result)
    return result


def pair_places(pair_block):
    base = pair_block * PAIRS
    first = lax.div(base, O)
    t = iota((1, PAIRS_PAD), 1) + (base - first * O)
    c = tenth(t)
    return first, t - c * O, c


def lane_rank(label, earlier=None):
    n = label.shape[1]
    same = iota((16, n), 0) == label
    if earlier is None:
        earlier = one_hot(iota((n, n), 0) < iota((n, n), 1))
    counts = jnp.dot(one_hot(same), earlier, preferred_element_type=F32)
    return jnp.sum(jnp.where(same, counts, 0.0), axis=0, keepdims=True).astype(I32)


def label_counts(occupied_row, value, labels):
    same = ((occupied_row ^ value) == labels) & (iota(labels.shape, 1) < O)
    return jnp.sum(jnp.where(same, 1.0, 0.0), axis=1, keepdims=True)


def places():
    row_block = lax.axis_index("row").astype(I32)
    pair_block = (lax.axis_index("col") * 4 + lax.axis_index("depth")).astype(I32)
    return row_block, pair_block


def start_copies(arrived, *pairs):
    copies = []
    for at, (source, target) in enumerate(pairs):
        copies.append(pltpu.make_async_copy(source, target, arrived.at[at]))
        copies[-1].start()
    return copies


def pack_columns_kernel(
    virtual_hbm,
    occupied_hbm,
    column_start_hbm,
    turn_hbm,
    integrals_hbm,
    packed,
    pair_label,
    table,
    integrals,
    virtual,
    occupied,
    column_start,
    turn,
    arrived,
):
    fetch = start_copies(
        arrived,
        (occupied_hbm, occupied),
        (virtual_hbm, virtual),
        (column_start_hbm, column_start),
        (turn_hbm, turn),
        (integrals_hbm, integrals),
    )
    row_block, pair_block = places()
    packed[...] = jnp.zeros((PACK, PAIRS_PAD), BF16)
    first, k_pair, c_pair = pair_places(pair_block)
    t = iota((1, 384), 1)
    c = tenth(t)
    looked_up = table_places(
        jnp.concatenate([k_pair, t - c * O], axis=1), jnp.concatenate([c_pair, c + 20], axis=1)
    )
    earlier = one_hot(iota((384, 384), 0) < iota((384, 384), 1))
    r = iota((COLUMNS, 128), 0)
    b = tenth(r)
    fetch[0].wait()
    occupied_row = table_row(occupied_values(occupied))
    for copy in fetch[1:4]:
        copy.wait()
    wpass = turn[1]
    blocks = COLUMNS // O
    own = virtual_values(virtual, column_start[0] + row_block * blocks, blocks)
    virtual_row = table_row(virtual_values(virtual, first, 20) + own)
    found = from_tables([occupied_row], virtual_row, looked_up)
    label = found[0] ^ found[1]
    here = label[:, :PAIRS_PAD].astype(F32).astype(BF16)
    pair_label[...] = jnp.broadcast_to(here, (16, PAIRS_PAD))
    table[...] = jnp.broadcast_to(occupied_row, (8, 128))
    rank = lane_rank(jnp.where(t < COLUMNS, label[:, PAIRS_PAD:], -1), earlier) - wpass * PACK
    chosen = one_hot((iota((PACK, 384), 0) == rank) & (t < COLUMNS))[:, :COLUMNS]
    column = down_table(occupied_row, r - b * O) ^ pick(own, b)
    column = column.astype(F32).astype(BF16)
    wide = jnp.concatenate([column] * (PAIRS_PAD // 128), axis=1)[:, :PAIRS]
    fetch[4].wait()
    masked = jnp.where(wide == here[:, :PAIRS], integrals[...], jnp.zeros((), BF16))
    packed[:, :PAIRS] = jnp.dot(chosen, masked, preferred_element_type=F32).astype(BF16)


def fullest(occupied_row, window, count, size):
    sub, lane = iota((16, 128), 0), iota((16, 128), 1)
    at, block = iota((128, 128), 0), iota((128, 128), 1)
    blocks = one_hot((at >= block * size) & (at < (block + 1) * size))
    virtuals = jnp.dot(one_hot((window == sub) & (lane < count)), blocks, preferred_element_type=F32)
    total = jnp.zeros((16, 128), F32)
    for h in range(8):
        total = total + label_counts(occupied_row, h, sub) * virtuals[h : h + 1]
    return total


def places_past(labels, lane, more_labels, earlier):
    past = jnp.dot(one_hot(labels == lane), more_labels, preferred_element_type=F32)
    before = jnp.dot(earlier, past.astype(BF16), preferred_element_type=F32)
    return jnp.where(past > 0.5, before, -1.0)


def pack_rows_kernel(
    virtual_hbm,
    row_start_hbm,
    column_start_hbm,
    turn_hbm,
    pair_label,
    table,
    amplitudes_hbm,
    rows_packed,
    unpack,
    column_label,
    row_places,
    more,
    more_labels,
    rows_more,
    column_more,
    left_over,
    spasses,
    wpasses,
    staged,
    amplitudes,
    virtual,
    row_start,
    column_start,
    turn,
    arrived,
):
    fetch = start_copies(
        arrived,
        (virtual_hbm, virtual),
        (row_start_hbm, row_start),
        (column_start_hbm, column_start),
        (turn_hbm, turn),
        (amplitudes_hbm, amplitudes),
    )
    row_block, _ = places()
    occupied_row = table[0:1]
    occupied_rank = lane_rank(jnp.where(iota((1, 128), 1) < O, occupied_row, -1))
    sub = iota((16, 128), 0)
    e = iota((OUT_PAD, 128), 0)
    t = jnp.concatenate([e + d * OUT for d in range(4)], axis=0)
    valid = jnp.concatenate([e] * 4, axis=0) < OUT
    b = tenth(t)
    occupied_here = down_table(occupied_row, t - b * O)
    rank_here = down_table(occupied_rank, t - b * O)
    p = iota((ROWS, 128), 0)
    p_block = tenth(p)
    row_column = down_table(occupied_row, p - p_block * O)
    for copy in fetch[:4]:
        copy.wait()
    spass, wpass = turn[0], turn[1]
    rank_here = rank_here - wpass * PACK

    own = virtual_values(virtual, row_start[0] + row_block * (ROWS // O), ROWS // O)
    t = iota((1, 896), 1)
    a = tenth(t)
    found = from_tables([occupied_row, occupied_rank], table_row(own), table_places(t - a * O, a))
    label_row = jnp.where(t < ROWS, found[0] ^ found[2], -1)
    before = jnp.zeros((16, 896), F32)
    for n, value in enumerate(own):
        before = before + jnp.where(a > n, label_counts(occupied_row, value, sub), 0.0)
    before = jnp.where(iota((16, 896), 0) == label_row, before, 0.0)
    rank = found[1] + jnp.sum(before, axis=0, keepdims=True).astype(I32) - spass * SLOTS
    slot = jnp.where((rank >= 0) & (rank < SLOTS) & (t < ROWS), rank, -1)
    at = iota((8, 896), 0)
    row_places[...] = jnp.where(at == 0, slot, jnp.where(at == 1, label_row, jnp.where(t < ROWS, rank, -1)))

    columns = virtual_values(virtual, column_start[0], VB)
    window = table_row(columns)
    row_window = table_row(virtual_values(virtual, row_start[0], VA))
    row_counts = fullest(occupied_row, row_window, VA, 8)
    most = jnp.max(row_counts).astype(I32)
    column_counts = fullest(occupied_row, window, VB, 3)
    wpasses[0] = lax.div(jnp.max(column_counts).astype(I32) + (PACK - 1), PACK)
    spasses[0] = lax.div(most + (SLOTS - 1), SLOTS)
    more[...] = jnp.zeros((8, 128), F32)

    @pl.when((most > SLOTS) & (most <= SLOTS + MORE))
    def _():
        t = iota((1, 2432), 1)
        b = tenth(t)
        found = from_tables([occupied_row], window, table_places(t - b * O, b))
        same = (iota((16, 2432), 0) == (found[0] ^ found[1])) & (t < VB * O)
        at, block = iota((2432, 128), 0), iota((2432, 128), 1)
        blocks = one_hot((at >= block * OUT) & (at < (block + 1) * OUT))
        in_block = jnp.dot(one_hot(same), blocks, preferred_element_type=F32)
        past = row_counts > SLOTS
        found = lax.dot_general(
            one_hot(past), in_block.astype(BF16), (((0,), (0,)), ((), ())), preferred_element_type=F32
        )
        fits = jnp.max(found).astype(I32) <= MORE_ROWS
        spasses[0] = jnp.where(fits, 1, spasses[0])
        mine = past & (iota((16, 128), 1) == row_block)
        mine = jnp.sum(jnp.where(mine, 1.0, 0.0), axis=1, keepdims=True)
        mine = jnp.where(fits, jnp.broadcast_to(mine, (16, 128)), 0.0)
        more[...] = jnp.broadcast_to(jnp.max(mine), (8, 128))
        more_labels[...] = jnp.zeros((128, 128), BF16)
        more_labels[:16] = mine.astype(BF16)

    left_over[0] = spasses[0] * wpasses[0] - 1

    x, core = lax.div(row_block, 2), lax.rem(row_block, 2)
    lane = iota((4 * OUT_PAD, 128), 1)
    key = iota((128, 128), 0)
    key_label = key & 7
    key_block = key >> 3
    for step in range(4):
        for half in range(2):
            shard = lax.rem(x - step + 4, 4) * 2 + half
            blocks = [
                virtual[jnp.minimum(column_start[0] + shard * (COLUMNS // O) + n, 599)] for n in range(3)
            ]
            labels = jnp.where(valid, occupied_here ^ pick(blocks, b), -1)
            before = jnp.zeros((128, 1), F32)
            for n in range(2):
                before = before + jnp.where(
                    key_block[:, :1] > n, label_counts(occupied_row, blocks[n], key_label), 0.0
                )
            before = jnp.where(key_block < 3, jnp.broadcast_to(before, (128, 128)), 0.0)
            at = jnp.dot(
                one_hot((lane == b * 8 + labels) & valid), before.astype(BF16), preferred_element_type=F32
            ).astype(I32)
            at = at + rank_here
            at = jnp.where((at >= 0) & (at < PACK) & valid, at + PACK * jnp.bitwise_xor(core, half), -1)
            rows = pl.ds((step * 2 + half) * 4 * OUT_PAD, 4 * OUT_PAD)
            unpack[rows, :] = one_hot(lane == at)
            column_label[rows, :] = labels.astype(F32).astype(BF16)

    row_column = row_column ^ pick(own, p_block)
    wide = jnp.concatenate([row_column.astype(F32).astype(BF16)] * (PAIRS_PAD // 128), axis=1)
    chosen = one_hot(iota((SLOT_LANES, 896), 0) == slot)[:, :ROWS]
    here = pair_label[0:1, :PAIRS]
    fetch[4].wait()
    masked = jnp.where(wide[:, :PAIRS] == here, amplitudes[...], jnp.zeros((), BF16))
    staged[...] = jnp.zeros((SLOT_LANES, PAIRS_PAD), F32)
    staged[:, :PAIRS] = jnp.dot(chosen, masked, preferred_element_type=F32)
    rows_packed[...] = jnp.transpose(staged[...]).astype(BF16)

    @pl.when(jnp.max(more[...]) > 0.0)
    def _():
        sub = iota((SLOT_LANES, 896), 0) & 15
        past = row_places[2:3, :] - SLOTS
        chosen = one_hot((sub == past) & (sub < MORE))[:, :ROWS]
        wide = jnp.concatenate([row_column.astype(F32).astype(BF16)] * (PAIRS_PAD // 128), axis=1)
        masked = jnp.where(
            wide[:, :PAIRS] == pair_label[0:1, :PAIRS], amplitudes[...], jnp.zeros((), BF16)
        )
        staged[:, :PAIRS] = jnp.dot(chosen, masked, preferred_element_type=F32)
        rows_more[...] = jnp.transpose(staged[...]).astype(BF16)
        n = 4 * OUT_PAD
        lane = iota((n, 128), 1)
        row, column = iota((n, n), 0), iota((n, n), 1)
        earlier = (column < row) & (lax.div(column, OUT_PAD) == lax.div(row, OUT_PAD))
        def block(shard, _):
            rows = pl.ds(pl.multiple_of(shard * n, n), n)
            labels = column_label[rows, :].astype(F32).astype(I32)
            column_more[rows, :] = places_past(labels, lane, more_labels[...], one_hot(earlier))
            return 0

        lax.fori_loop(0, 8, block, 0)


def contract_kernel(
    steps, unpack, column_label, pair_label, rows_packed, more, rows_more, column_more, *refs
):
    shards, (sums, coded_rows, held, sent) = refs[: 2 * len(steps)], refs[-4:]
    any_more = jnp.max(more[...]) > 0.0
    x = lax.div(places()[0], 2)
    rows = rows_packed[...]
    here = pair_label[0:1]
    n = 8 * OUT_PAD
    lane = iota((n, SLOT_LANES), 1)
    copies = []
    for place, step in enumerate(steps):
        at = pl.ds(step * n, n)

        pair = jnp.concatenate([shards[2 * place][...], shards[2 * place + 1][...]], axis=0)
        spread = jnp.dot(unpack[at, :], pair, preferred_element_type=F32).astype(BF16)
        wide = jnp.concatenate([column_label[at, :]] * (PAIRS_PAD // 128), axis=1)
        masked = jnp.where(wide == here, spread, jnp.zeros((), BF16))
        held[...] = jnp.dot(masked, rows, preferred_element_type=F32)

        @pl.when(any_more)
        def _():
            def block(d, _):
                at = pl.ds(pl.multiple_of(step * n + d * OUT_PAD, OUT_PAD), OUT_PAD)
                spread = jnp.dot(unpack[at, :], pair, preferred_element_type=F32).astype(BF16)
                wide = jnp.concatenate([column_label[at, :]] * (PAIRS_PAD // 128), axis=1)
                masked = jnp.where(wide == here, spread, jnp.zeros((), BF16))
                past = jnp.dot(masked, rows_more[...], preferred_element_type=F32)
                to = column_more[at, :].astype(I32)
                lane = iota((OUT_PAD, SLOT_LANES), 1)
                past = jnp.where((to >= 0) & ((to & 7) == (lane >> 4)), past, 0.0)
                target = (8 - OUT_PAD + OUT) + (to >> 3)
                moved = lax.dot_general(
                    jnp.where((to >= 0) & (lane == target), 1.0, 0.0),
                    past,
                    (((0,), (0,)), ((), ())),
                    precision=lax.Precision.HIGHEST,
                    preferred_element_type=F32,
                )
                pad = pl.ds(pl.multiple_of((d + 1) * OUT_PAD - 8, 8), 8)
                held[pad, :] = held[pad, :] + moved[:8]
                return 0

            lax.fori_loop(0, 8, block, 0)

        part = held[...]
        top = jnp.max(jnp.abs(part), axis=1, keepdims=True)
        exponent = jnp.ceil(jnp.log2(jnp.maximum(top, 2.0**-120)) * STEPS)
        back = jnp.exp2(15.0 - exponent * (1.0 / STEPS))
        coded = jnp.clip(jnp.round(part * back), -32767.0, 32767.0)
        coded = jnp.where(lane == SLOTS, exponent, coded).astype(I32).astype(jnp.int16)
        for d in range(8):
            coded_rows[place * 8 + d] = coded[d * OUT_PAD : (d + 1) * OUT_PAD]
        copy = pltpu.make_async_copy(
            coded_rows.at[pl.ds(place * 8, 8)],
            sums.at[pl.ds(lax.rem(x - step + 4, 4) * 8, 8)],
            sent.at[place],
        )
        copy.start()
        copies.append(copy)
    for copy in copies:
        copy.wait()


def place_kernel(
    virtual,
    occupied,
    column_start,
    row_places,
    more,
    more_labels,
    chosen,
    row_label,
    column_label,
    own_more,
):
    _, place = places()
    occupied_row = table_row(occupied_values(occupied))
    first = lax.div(place * OUT, O)
    t = iota((OUT_PAD, 128), 0) + (place * OUT - first * O)
    c = tenth(t)
    values = virtual_values(virtual, column_start[0] + first, 2)
    labels = down_table(occupied_row, t - c * O) ^ pick(values, c)
    column_label[...] = labels.astype(F32)

    @pl.when(jnp.max(more[...]) > 0.0)
    def _():
        row, column = iota((OUT_PAD, OUT_PAD), 0), iota((OUT_PAD, OUT_PAD), 1)
        e, lane = iota((OUT_PAD, 128), 0), iota((OUT_PAD, 128), 1)
        valid = jnp.where(e < OUT, labels, -1)
        own_more[...] = places_past(valid, lane, more_labels[...], one_hot(column < row))

    chosen[...] = one_hot(iota((SLOT_LANES, 896), 0) == row_places[0:1, :])
    row_label[...] = jnp.broadcast_to(row_places[1:2, :].astype(F32), (8, 896))


def spread_kernel(chosen, row_label, column_label, own_more, row_places, more, parts, others, out, held):
    total = jnp.zeros((OUT_PAD, SLOT_LANES), F32)
    for d in range(parts.shape[0]):
        part = parts[d].astype(I32).astype(F32)
        total = total + part * jnp.exp2(part[:, SLOTS:] * (1.0 / STEPS) - 15.0)
    lane = iota((OUT_PAD, SLOT_LANES), 1)
    total = jnp.where(lane < SLOTS, total, 0.0).astype(BF16)
    held[...] = jnp.dot(total, chosen[...], preferred_element_type=F32)

    @pl.when(jnp.max(more[...]) > 0.0)
    def _():
        to = own_more[...].astype(I32)
        source = one_hot((to >= 0) & (lane == OUT + (to >> 3)))[:, :OUT_PAD]
        past = jnp.dot(source, total, preferred_element_type=F32)
        past = jnp.where((to >= 0) & ((to & 7) == (lane >> 4)), past, 0.0).astype(BF16)
        sub = iota((SLOT_LANES, 896), 0) & 15
        moved = one_hot((sub == row_places[2:3, :] - SLOTS) & (sub < MORE))
        held[...] = held[...] + jnp.dot(past, moved, preferred_element_type=F32)

    wide = jnp.concatenate([column_label[...]] * 7, axis=1)
    spread = jnp.where(wide == row_label[0:1], held[...], 0.0).astype(BF16)
    out[...] = spread[:OUT, :ROWS] + others[...]


SMEM = pl.BlockSpec(memory_space=pltpu.SMEM)
VMEM = pl.BlockSpec(memory_space=pltpu.VMEM)
ANY = pl.BlockSpec(memory_space=pl.ANY)
HBM = pl.BlockSpec(memory_space=pltpu.HBM)


def call(kernel, name, ins, outs, scratch=(), flops=0, moved=0, out_specs=None, aliases=None):
    return pl.pallas_call(
        kernel,
        name=name,
        in_specs=ins,
        out_specs=out_specs or ([VMEM] * len(outs) if len(outs) > 1 else VMEM),
        out_shape=outs if len(outs) > 1 else outs[0],
        scratch_shapes=scratch,
        input_output_aliases=aliases or {},
        compiler_params=pltpu.CompilerParams(vmem_limit_bytes=VMEM_LIMIT),
        cost_estimate=pl.CostEstimate(flops=flops, bytes_accessed=moved, transcendentals=0),
    )


def shape(dims, kind):
    return jax.ShapeDtypeStruct(dims, kind)


def after(value, *others):
    return lax.optimization_barrier((value, *others))[0]


def one_pass(amplitudes, integrals, virtual, occupied, row_start, column_start, turn, others):
    packed, pair_label, table = call(
        pack_columns_kernel,
        "pack_columns",
        [HBM] * 5,
        [
            shape((PACK, PAIRS_PAD), BF16),
            shape((16, PAIRS_PAD), BF16),
            shape((8, 128), I32),
        ],
        [
            pltpu.VMEM((COLUMNS, PAIRS), BF16),
            pltpu.SMEM((600,), I32),
            pltpu.SMEM((O,), I32),
            pltpu.SMEM((1,), I32),
            pltpu.SMEM((2,), I32),
            pltpu.SemaphoreType.DMA((5,)),
        ],
        flops=2 * 8 * PACK * COLUMNS * PAIRS,
        moved=2 * PAIRS * (COLUMNS + PACK),
    )(virtual, occupied, column_start, turn, integrals.T)

    def along_x(step):
        return lax.ppermute(packed, "row", [(i, (i + 2 * step) % 8) for i in range(8)])

    def to_sibling(block):
        return lax.ppermute(block, "row", [(i, i ^ 1) for i in range(8)])

    from_1, from_3, from_2 = along_x(1), along_x(3), along_x(2)
    own_other = to_sibling(packed)
    (
        rows_packed,
        unpack,
        column_label,
        row_places,
        more,
        more_labels,
        rows_more,
        column_more,
        *passes,
    ) = call(
        pack_rows_kernel,
        "pack_rows",
        [HBM] * 4 + [VMEM] * 2 + [HBM],
        [
            shape((PAIRS_PAD, SLOT_LANES), BF16),
            shape((8 * 4 * OUT_PAD, 128), BF16),
            shape((8 * 4 * OUT_PAD, 128), BF16),
            shape((8, 896), I32),
            shape((8, 128), F32),
            shape((128, 128), BF16),
            shape((PAIRS_PAD, SLOT_LANES), BF16),
            shape((8 * 4 * OUT_PAD, 128), F32),
            shape((1,), I32),
            shape((1,), I32),
            shape((1,), I32),
        ],
        [
            pltpu.VMEM((SLOT_LANES, PAIRS_PAD), F32),
            pltpu.VMEM((ROWS, PAIRS), BF16),
            pltpu.SMEM((600,), I32),
            pltpu.SMEM((1,), I32),
            pltpu.SMEM((1,), I32),
            pltpu.SMEM((2,), I32),
            pltpu.SemaphoreType.DMA((5,)),
        ],
        flops=2 * SLOT_LANES * ROWS * PAIRS,
        moved=2 * PAIRS * ROWS * 3,
        out_specs=[VMEM] * 8 + [SMEM] * 3,
    )(virtual, row_start, column_start, turn, pair_label, table, amplitudes)

    def contract(steps, shards, sums):
        held = [] if sums is None else [sums]
        return call(
            functools.partial(contract_kernel, steps),
            "contract_" + "_".join(map(str, steps)),
            [VMEM] * (7 + len(shards)) + [ANY] * len(held),
            [shape((32, OUT_PAD, SLOT_LANES), jnp.int16)],
            [
                pltpu.VMEM((8 * len(steps), OUT_PAD, SLOT_LANES), jnp.int16),
                pltpu.VMEM((8 * OUT_PAD, SLOT_LANES), F32),
                pltpu.SemaphoreType.DMA((len(steps),)),
            ],
            flops=2 * 640 * len(steps) * PAIRS_PAD * 256,
            moved=2 * len(shards) * PACK * PAIRS_PAD,
            out_specs=ANY,
            aliases={} if sums is None else {7 + len(shards): 0},
        )(
            unpack,
            column_label,
            pair_label,
            rows_packed,
            more,
            rows_more,
            column_more,
            *shards,
            *held,
        )

    *found, own_more = call(
        place_kernel,
        "place",
        [SMEM] * 3 + [VMEM] * 3,
        [
            shape((SLOT_LANES, 896), BF16),
            shape((8, 896), F32),
            shape((OUT_PAD, 128), F32),
            shape((OUT_PAD, 128), F32),
        ],
    )(virtual, occupied, column_start, row_places, more, more_labels)
    from_1, from_3, rows_packed, *found = lax.optimization_barrier((from_1, from_3, rows_packed, *found))
    other_1, other_3 = to_sibling(from_1), to_sibling(from_3)
    sums = contract((0,), (packed, own_other), None)
    from_2, sums = lax.optimization_barrier((from_2, sums))
    other_2 = to_sibling(from_2)
    sums = contract((1, 3), (from_1, other_1, from_3, other_3), sums)
    sums = contract((2,), (from_2, other_2), sums)
    sums, *passes = lax.optimization_barrier((sums, *passes))
    parts = lax.all_to_all(sums, ("col", "depth"), 0, 0)
    return call(
        spread_kernel,
        "spread",
        [VMEM] * 8,
        [shape((OUT, ROWS), BF16)],
        [pltpu.VMEM((OUT_PAD, 896), F32)],
        flops=2 * OUT * ROWS * 128,
        moved=2 * 32 * OUT_PAD * SLOT_LANES,
    )(*found, own_more, row_places, more, parts, others(*passes))


def body(amplitudes, integrals, virtual_irrep, occupied_irrep, row_start, column_start):
    run = functools.partial(
        one_pass, amplitudes, integrals, virtual_irrep, occupied_irrep, row_start, column_start
    )
    def more(state):
        return state[0][0] > 0

    def again(state):
        left, out, spasses, wpasses = state
        turn = jnp.concatenate([lax.div(left, wpasses), lax.rem(left, wpasses)])
        return left - 1, run(turn, lambda *_: out), spasses, wpasses

    def other_passes(left, spasses, wpasses):
        nothing = jnp.zeros((OUT, ROWS), BF16)
        return lax.while_loop(more, again, (left, nothing, spasses, wpasses))[1]

    return run(jnp.zeros((2,), I32), other_passes)


def solution(mesh):
    return jax.shard_map(
        body,
        mesh=mesh,
        in_specs=(P("row", ("col", "depth")), P(("col", "depth"), "row"), P(), P(), P(), P()),
        out_specs=P(("col", "depth"), "row"),
        check_vma=False,
    )
```

```python
import functools

import jax
import jax.numpy as jnp
from jax import lax
from jax.experimental import pallas as pl
from jax.experimental.pallas import tpu as pltpu
from jax.sharding import PartitionSpec as P

O = 100
VA = 64
VB = 24
PAIRS = 1875
PAIRS_PAD = 1920
ROWS = 800
COLUMNS = 300
OUT = 75
OUT_PAD = 80
SLOTS = 127
SLOT_LANES = 128
MORE = 15
MORE_ROWS = (OUT_PAD - OUT) * 8
PACK = 64
F32 = jnp.float32
BF16 = jnp.bfloat16
I32 = jnp.int32
STEPS = 256.0
VMEM_LIMIT = 40 * 1024 * 1024


def iota(shape, dim):
    return lax.broadcasted_iota(I32, shape, dim)


def tenth(t):
    return (t * 5243) >> 19


def table_row(values):
    lane = iota((1, 128), 1)
    row = jnp.zeros((1, 128), I32)
    for at, value in enumerate(values):
        row = jnp.where(lane == at, value, row)
    return row


def occupied_values(occupied):
    return [occupied[k] for k in range(O)]


def virtual_values(virtual, start, count):
    return [virtual[jnp.minimum(start + n, 599)] for n in range(count)]


def one_hot(flags):
    return jnp.where(flags, 1.0, 0.0).astype(BF16)


def from_tables(occupied_rows, virtual_row, k, c):
    n, count = k.shape[1], len(occupied_rows)
    sub = iota((16, 128), 0)
    left = jnp.zeros((16, 128), I32)
    for at, row in enumerate(occupied_rows):
        left = jnp.where(sub == at, row, left)
    right = jnp.where(sub[:, :32] == count, virtual_row[:, :32], 0)
    left = jnp.concatenate([left.astype(F32), right.astype(F32)], axis=1).astype(BF16)
    places = jnp.concatenate(
        [one_hot(iota((128, n), 0) == k), one_hot(iota((32, n), 0) == c)], axis=0
    )
    found = jnp.dot(left, places, preferred_element_type=F32).astype(I32)
    return [found[at : at + 1] for at in range(count + 1)]


def down_table(row, k):
    table = jnp.broadcast_to(row.astype(F32), (128, 128)).astype(BF16)
    places = one_hot(iota(k.shape, 1) == k)
    found = lax.dot_general(
        places, table, (((1,), (1,)), ((), ())), preferred_element_type=F32
    )
    return found.astype(I32)


def pick(values, at):
    result = jnp.full(at.shape, values[0], I32)
    for n, value in enumerate(values[1:], 1):
        result = jnp.where(at == n, value, result)
    return result


def pair_places(pair_block):
    base = pair_block * PAIRS
    first = lax.div(base, O)
    t = iota((1, PAIRS_PAD), 1) + (base - first * O)
    c = tenth(t)
    return first, t - c * O, c


def lane_rank(label):
    n = label.shape[1]
    same = iota((16, n), 0) == label
    earlier = one_hot(iota((n, n), 0) < iota((n, n), 1))
    counts = jnp.dot(one_hot(same), earlier, preferred_element_type=F32)
    return jnp.sum(jnp.where(same, counts, 0.0), axis=0, keepdims=True).astype(I32)


def label_counts(occupied_row, value, labels):
    same = ((occupied_row ^ value) == labels) & (iota(labels.shape, 1) < O)
    return jnp.sum(jnp.where(same, 1.0, 0.0), axis=1, keepdims=True)


def places():
    row_block = lax.axis_index("row").astype(I32)
    pair_block = (lax.axis_index("col") * 4 + lax.axis_index("depth")).astype(I32)
    return row_block, pair_block


def start_copies(arrived, *pairs):
    copies = []
    for at, (source, target) in enumerate(pairs):
        copies.append(pltpu.make_async_copy(source, target, arrived.at[at]))
        copies[-1].start()
    return copies


def pack_columns_kernel(
    virtual_hbm,
    occupied_hbm,
    column_start_hbm,
    turn_hbm,
    integrals_hbm,
    packed,
    pair_label,
    table,
    integrals,
    virtual,
    occupied,
    column_start,
    turn,
    arrived,
):
    fetch = start_copies(
        arrived,
        (occupied_hbm, occupied),
        (virtual_hbm, virtual),
        (column_start_hbm, column_start),
        (turn_hbm, turn),
        (integrals_hbm, integrals),
    )
    row_block, pair_block = places()
    packed[...] = jnp.zeros((PACK, PAIRS_PAD), BF16)
    first, k_pair, c_pair = pair_places(pair_block)
    fetch[0].wait()
    occupied_row = table_row(occupied_values(occupied))
    for copy in fetch[1:4]:
        copy.wait()
    wpass = turn[1]
    blocks = COLUMNS // O
    own = virtual_values(virtual, column_start[0] + row_block * blocks, blocks)
    virtual_row = table_row(virtual_values(virtual, first, 20) + own)
    t = iota((1, 384), 1)
    c = tenth(t)
    found = from_tables(
        [occupied_row],
        virtual_row,
        jnp.concatenate([k_pair, t - c * O], axis=1),
        jnp.concatenate([c_pair, c + 20], axis=1),
    )
    label = found[0] ^ found[1]
    here = label[:, :PAIRS_PAD].astype(F32).astype(BF16)
    pair_label[...] = jnp.broadcast_to(here, (16, PAIRS_PAD))
    table[...] = jnp.broadcast_to(occupied_row, (8, 128))
    rank = lane_rank(jnp.where(t < COLUMNS, label[:, PAIRS_PAD:], -1)) - wpass * PACK
    chosen = one_hot((iota((PACK, 384), 0) == rank) & (t < COLUMNS))[:, :COLUMNS]
    r = iota((COLUMNS, 128), 0)
    b = tenth(r)
    column = down_table(occupied_row, r - b * O) ^ pick(own, b)
    column = column.astype(F32).astype(BF16)
    wide = jnp.concatenate([column] * (PAIRS_PAD // 128), axis=1)[:, :PAIRS]
    fetch[4].wait()
    masked = jnp.where(wide == here[:, :PAIRS], integrals[...], jnp.zeros((), BF16))
    packed[:, :PAIRS] = jnp.dot(chosen, masked, preferred_element_type=F32).astype(BF16)


def fullest(occupied_row, window, count, size):
    sub, lane = iota((16, 128), 0), iota((16, 128), 1)
    at, block = iota((128, 128), 0), iota((128, 128), 1)
    blocks = one_hot((at >= block * size) & (at < (block + 1) * size))
    virtuals = jnp.dot(one_hot((window == sub) & (lane < count)), blocks, preferred_element_type=F32)
    total = jnp.zeros((16, 128), F32)
    for h in range(8):
        total = total + label_counts(occupied_row, h, sub) * virtuals[h : h + 1]
    return total


def places_past(labels, lane, more_labels, earlier):
    past = jnp.dot(one_hot(labels == lane), more_labels, preferred_element_type=F32)
    before = jnp.dot(earlier, past.astype(BF16), preferred_element_type=F32)
    return jnp.where(past > 0.5, before, -1.0)


def pack_rows_kernel(
    virtual_hbm,
    row_start_hbm,
    column_start_hbm,
    turn_hbm,
    pair_label,
    table,
    amplitudes_hbm,
    rows_packed,
    unpack,
    column_label,
    row_places,
    more,
    more_labels,
    rows_more,
    column_more,
    left_over,
    spasses,
    wpasses,
    staged,
    amplitudes,
    virtual,
    row_start,
    column_start,
    turn,
    arrived,
):
    fetch = start_copies(
        arrived,
        (virtual_hbm, virtual),
        (row_start_hbm, row_start),
        (column_start_hbm, column_start),
        (turn_hbm, turn),
        (amplitudes_hbm, amplitudes),
    )
    row_block, _ = places()
    occupied_row = table[0:1]
    occupied_rank = lane_rank(jnp.where(iota((1, 128), 1) < O, occupied_row, -1))
    sub = iota((16, 128), 0)
    e = iota((OUT_PAD, 128), 0)
    t = jnp.concatenate([e + d * OUT for d in range(4)], axis=0)
    valid = jnp.concatenate([e] * 4, axis=0) < OUT
    b = tenth(t)
    occupied_here = down_table(occupied_row, t - b * O)
    rank_here = down_table(occupied_rank, t - b * O)
    p = iota((ROWS, 128), 0)
    p_block = tenth(p)
    row_column = down_table(occupied_row, p - p_block * O)
    for copy in fetch[:4]:
        copy.wait()
    spass, wpass = turn[0], turn[1]
    rank_here = rank_here - wpass * PACK

    own = virtual_values(virtual, row_start[0] + row_block * (ROWS // O), ROWS // O)
    t = iota((1, 896), 1)
    a = tenth(t)
    found = from_tables([occupied_row, occupied_rank], table_row(own), t - a * O, a)
    label_row = jnp.where(t < ROWS, found[0] ^ found[2], -1)
    before = jnp.zeros((16, 896), F32)
    for n, value in enumerate(own):
        before = before + jnp.where(a > n, label_counts(occupied_row, value, sub), 0.0)
    before = jnp.where(iota((16, 896), 0) == label_row, before, 0.0)
    rank = found[1] + jnp.sum(before, axis=0, keepdims=True).astype(I32) - spass * SLOTS
    slot = jnp.where((rank >= 0) & (rank < SLOTS) & (t < ROWS), rank, -1)
    at = iota((8, 896), 0)
    row_places[...] = jnp.where(at == 0, slot, jnp.where(at == 1, label_row, jnp.where(t < ROWS, rank, -1)))

    columns = virtual_values(virtual, column_start[0], VB)
    window = table_row(columns)
    row_window = table_row(virtual_values(virtual, row_start[0], VA))
    row_counts = fullest(occupied_row, row_window, VA, 8)
    most = jnp.max(row_counts).astype(I32)
    column_counts = fullest(occupied_row, window, VB, 3)
    wpasses[0] = lax.div(jnp.max(column_counts).astype(I32) + (PACK - 1), PACK)
    spasses[0] = lax.div(most + (SLOTS - 1), SLOTS)
    more[...] = jnp.zeros((8, 128), F32)

    @pl.when((most > SLOTS) & (most <= SLOTS + MORE))
    def _():
        t = iota((1, 2432), 1)
        b = tenth(t)
        found = from_tables([occupied_row], window, t - b * O, b)
        same = (iota((16, 2432), 0) == (found[0] ^ found[1])) & (t < VB * O)
        at, block = iota((2432, 128), 0), iota((2432, 128), 1)
        blocks = one_hot((at >= block * OUT) & (at < (block + 1) * OUT))
        in_block = jnp.dot(one_hot(same), blocks, preferred_element_type=F32)
        past = row_counts > SLOTS
        found = lax.dot_general(
            one_hot(past), in_block.astype(BF16), (((0,), (0,)), ((), ())), preferred_element_type=F32
        )
        fits = jnp.max(found).astype(I32) <= MORE_ROWS
        spasses[0] = jnp.where(fits, 1, spasses[0])
        mine = past & (iota((16, 128), 1) == row_block)
        mine = jnp.sum(jnp.where(mine, 1.0, 0.0), axis=1, keepdims=True)
        mine = jnp.where(fits, jnp.broadcast_to(mine, (16, 128)), 0.0)
        more[...] = jnp.broadcast_to(jnp.max(mine), (8, 128))
        more_labels[...] = jnp.zeros((128, 128), BF16)
        more_labels[:16] = mine.astype(BF16)

    left_over[0] = spasses[0] * wpasses[0] - 1

    x, core = lax.div(row_block, 2), lax.rem(row_block, 2)
    lane = iota((4 * OUT_PAD, 128), 1)
    key = iota((128, 128), 0)
    key_label = key & 7
    key_block = key >> 3
    for step in range(4):
        for half in range(2):
            shard = lax.rem(x - step + 4, 4) * 2 + half
            blocks = [
                virtual[jnp.minimum(column_start[0] + shard * (COLUMNS // O) + n, 599)] for n in range(3)
            ]
            labels = jnp.where(valid, occupied_here ^ pick(blocks, b), -1)
            before = jnp.zeros((128, 1), F32)
            for n in range(2):
                before = before + jnp.where(
                    key_block[:, :1] > n, label_counts(occupied_row, blocks[n], key_label), 0.0
                )
            before = jnp.where(key_block < 3, jnp.broadcast_to(before, (128, 128)), 0.0)
            at = jnp.dot(
                one_hot((lane == b * 8 + labels) & valid), before.astype(BF16), preferred_element_type=F32
            ).astype(I32)
            at = at + rank_here
            at = jnp.where((at >= 0) & (at < PACK) & valid, at + PACK * jnp.bitwise_xor(core, half), -1)
            rows = pl.ds((step * 2 + half) * 4 * OUT_PAD, 4 * OUT_PAD)
            unpack[rows, :] = one_hot(lane == at)
            column_label[rows, :] = labels.astype(F32).astype(BF16)

    row_column = row_column ^ pick(own, p_block)
    wide = jnp.concatenate([row_column.astype(F32).astype(BF16)] * (PAIRS_PAD // 128), axis=1)
    chosen = one_hot(iota((SLOT_LANES, 896), 0) == slot)[:, :ROWS]
    here = pair_label[0:1, :PAIRS]
    fetch[4].wait()
    masked = jnp.where(wide[:, :PAIRS] == here, amplitudes[...], jnp.zeros((), BF16))
    staged[...] = jnp.zeros((SLOT_LANES, PAIRS_PAD), F32)
    staged[:, :PAIRS] = jnp.dot(chosen, masked, preferred_element_type=F32)
    rows_packed[...] = jnp.transpose(staged[...]).astype(BF16)

    @pl.when(jnp.max(more[...]) > 0.0)
    def _():
        sub = iota((SLOT_LANES, 896), 0) & 15
        past = row_places[2:3, :] - SLOTS
        chosen = one_hot((sub == past) & (sub < MORE))[:, :ROWS]
        wide = jnp.concatenate([row_column.astype(F32).astype(BF16)] * (PAIRS_PAD // 128), axis=1)
        masked = jnp.where(
            wide[:, :PAIRS] == pair_label[0:1, :PAIRS], amplitudes[...], jnp.zeros((), BF16)
        )
        staged[:, :PAIRS] = jnp.dot(chosen, masked, preferred_element_type=F32)
        rows_more[...] = jnp.transpose(staged[...]).astype(BF16)
        n = 4 * OUT_PAD
        lane = iota((n, 128), 1)
        row, column = iota((n, n), 0), iota((n, n), 1)
        earlier = (column < row) & (lax.div(column, OUT_PAD) == lax.div(row, OUT_PAD))
        for shard in range(8):
            rows = pl.ds(shard * n, n)
            labels = column_label[rows, :].astype(F32).astype(I32)
            column_more[rows, :] = places_past(labels, lane, more_labels[...], one_hot(earlier))


def contract_kernel(
    steps, unpack, column_label, pair_label, rows_packed, more, rows_more, column_more, *refs
):
    shards, (sums, coded_rows, held, sent) = refs[: 2 * len(steps)], refs[-4:]
    any_more = jnp.max(more[...]) > 0.0
    x = lax.div(places()[0], 2)
    rows = rows_packed[...]
    here = pair_label[0:1]
    n = 8 * OUT_PAD
    lane = iota((n, SLOT_LANES), 1)
    copies = []
    for place, step in enumerate(steps):
        at = pl.ds(step * n, n)

        pair = jnp.concatenate([shards[2 * place][...], shards[2 * place + 1][...]], axis=0)
        spread = jnp.dot(unpack[at, :], pair, preferred_element_type=F32).astype(BF16)
        wide = jnp.concatenate([column_label[at, :]] * (PAIRS_PAD // 128), axis=1)
        masked = jnp.where(wide == here, spread, jnp.zeros((), BF16))
        held[...] = jnp.dot(masked, rows, preferred_element_type=F32)

        @pl.when(any_more)
        def _():
            past = jnp.dot(masked, rows_more[...], preferred_element_type=F32)
            to = column_more[at, :].astype(I32)
            past = jnp.where((to >= 0) & ((to & 7) == (lane >> 4)), past, 0.0)
            target = lax.div(iota((n, 128), 0), OUT_PAD) * 8 + (8 - OUT_PAD + OUT) + (to >> 3)
            moved = lax.dot_general(
                jnp.where((to >= 0) & (lane == target), 1.0, 0.0),
                past,
                (((0,), (0,)), ((), ())),
                precision=lax.Precision.HIGHEST,
                preferred_element_type=F32,
            )
            for d in range(8):
                pad = pl.ds((d + 1) * OUT_PAD - 8, 8)
                held[pad, :] = held[pad, :] + moved[d * 8 : (d + 1) * 8]

        part = held[...]
        top = jnp.max(jnp.abs(part), axis=1, keepdims=True)
        exponent = jnp.ceil(jnp.log2(jnp.maximum(top, 2.0**-120)) * STEPS)
        back = jnp.exp2(15.0 - exponent * (1.0 / STEPS))
        coded = jnp.clip(jnp.round(part * back), -32767.0, 32767.0)
        coded = jnp.where(lane == SLOTS, exponent, coded).astype(I32).astype(jnp.int16)
        for d in range(8):
            coded_rows[place * 8 + d] = coded[d * OUT_PAD : (d + 1) * OUT_PAD]
        copy = pltpu.make_async_copy(
            coded_rows.at[pl.ds(place * 8, 8)],
            sums.at[pl.ds(lax.rem(x - step + 4, 4) * 8, 8)],
            sent.at[place],
        )
        copy.start()
        copies.append(copy)
    for copy in copies:
        copy.wait()


def place_kernel(
    virtual,
    occupied,
    column_start,
    row_places,
    more,
    more_labels,
    chosen,
    row_label,
    column_label,
    own_more,
):
    _, place = places()
    occupied_row = table_row(occupied_values(occupied))
    first = lax.div(place * OUT, O)
    t = iota((OUT_PAD, 128), 0) + (place * OUT - first * O)
    c = tenth(t)
    values = virtual_values(virtual, column_start[0] + first, 2)
    labels = down_table(occupied_row, t - c * O) ^ pick(values, c)
    column_label[...] = labels.astype(F32)

    @pl.when(jnp.max(more[...]) > 0.0)
    def _():
        row, column = iota((OUT_PAD, OUT_PAD), 0), iota((OUT_PAD, OUT_PAD), 1)
        e, lane = iota((OUT_PAD, 128), 0), iota((OUT_PAD, 128), 1)
        valid = jnp.where(e < OUT, labels, -1)
        own_more[...] = places_past(valid, lane, more_labels[...], one_hot(column < row))

    chosen[...] = one_hot(iota((SLOT_LANES, 896), 0) == row_places[0:1, :])
    row_label[...] = jnp.broadcast_to(row_places[1:2, :].astype(F32), (8, 896))


def spread_kernel(chosen, row_label, column_label, own_more, row_places, more, parts, others, out, held):
    total = jnp.zeros((OUT_PAD, SLOT_LANES), F32)
    for d in range(parts.shape[0]):
        part = parts[d].astype(I32).astype(F32)
        total = total + part * jnp.exp2(part[:, SLOTS:] * (1.0 / STEPS) - 15.0)
    lane = iota((OUT_PAD, SLOT_LANES), 1)
    total = jnp.where(lane < SLOTS, total, 0.0).astype(BF16)
    held[...] = jnp.dot(total, chosen[...], preferred_element_type=F32)

    @pl.when(jnp.max(more[...]) > 0.0)
    def _():
        to = own_more[...].astype(I32)
        source = one_hot((to >= 0) & (lane == OUT + (to >> 3)))[:, :OUT_PAD]
        past = jnp.dot(source, total, preferred_element_type=F32)
        past = jnp.where((to >= 0) & ((to & 7) == (lane >> 4)), past, 0.0).astype(BF16)
        sub = iota((SLOT_LANES, 896), 0) & 15
        moved = one_hot((sub == row_places[2:3, :] - SLOTS) & (sub < MORE))
        held[...] = held[...] + jnp.dot(past, moved, preferred_element_type=F32)

    wide = jnp.concatenate([column_label[...]] * 7, axis=1)
    spread = jnp.where(wide == row_label[0:1], held[...], 0.0).astype(BF16)
    out[...] = spread[:OUT, :ROWS] + others[...]


SMEM = pl.BlockSpec(memory_space=pltpu.SMEM)
VMEM = pl.BlockSpec(memory_space=pltpu.VMEM)
ANY = pl.BlockSpec(memory_space=pl.ANY)
HBM = pl.BlockSpec(memory_space=pltpu.HBM)


def call(kernel, name, ins, outs, scratch=(), flops=0, moved=0, out_specs=None, aliases=None):
    return pl.pallas_call(
        kernel,
        name=name,
        in_specs=ins,
        out_specs=out_specs or ([VMEM] * len(outs) if len(outs) > 1 else VMEM),
        out_shape=outs if len(outs) > 1 else outs[0],
        scratch_shapes=scratch,
        input_output_aliases=aliases or {},
        compiler_params=pltpu.CompilerParams(vmem_limit_bytes=VMEM_LIMIT),
        cost_estimate=pl.CostEstimate(flops=flops, bytes_accessed=moved, transcendentals=0),
    )


def shape(dims, kind):
    return jax.ShapeDtypeStruct(dims, kind)


def after(value, *others):
    return lax.optimization_barrier((value, *others))[0]


def one_pass(amplitudes, integrals, virtual, occupied, row_start, column_start, turn, others):
    packed, pair_label, table = call(
        pack_columns_kernel,
        "pack_columns",
        [HBM] * 5,
        [
            shape((PACK, PAIRS_PAD), BF16),
            shape((16, PAIRS_PAD), BF16),
            shape((8, 128), I32),
        ],
        [
            pltpu.VMEM((COLUMNS, PAIRS), BF16),
            pltpu.SMEM((600,), I32),
            pltpu.SMEM((O,), I32),
            pltpu.SMEM((1,), I32),
            pltpu.SMEM((2,), I32),
            pltpu.SemaphoreType.DMA((5,)),
        ],
        flops=2 * 8 * PACK * COLUMNS * PAIRS,
        moved=2 * PAIRS * (COLUMNS + PACK),
    )(virtual, occupied, column_start, turn, integrals.T)

    def along_x(step):
        return lax.ppermute(packed, "row", [(i, (i + 2 * step) % 8) for i in range(8)])

    def to_sibling(block):
        return lax.ppermute(block, "row", [(i, i ^ 1) for i in range(8)])

    from_1, from_3, from_2 = along_x(1), along_x(3), along_x(2)
    own_other = to_sibling(packed)
    (
        rows_packed,
        unpack,
        column_label,
        row_places,
        more,
        more_labels,
        rows_more,
        column_more,
        *passes,
    ) = call(
        pack_rows_kernel,
        "pack_rows",
        [HBM] * 4 + [VMEM] * 2 + [HBM],
        [
            shape((PAIRS_PAD, SLOT_LANES), BF16),
            shape((8 * 4 * OUT_PAD, 128), BF16),
            shape((8 * 4 * OUT_PAD, 128), BF16),
            shape((8, 896), I32),
            shape((8, 128), F32),
            shape((128, 128), BF16),
            shape((PAIRS_PAD, SLOT_LANES), BF16),
            shape((8 * 4 * OUT_PAD, 128), F32),
            shape((1,), I32),
            shape((1,), I32),
            shape((1,), I32),
        ],
        [
            pltpu.VMEM((SLOT_LANES, PAIRS_PAD), F32),
            pltpu.VMEM((ROWS, PAIRS), BF16),
            pltpu.SMEM((600,), I32),
            pltpu.SMEM((1,), I32),
            pltpu.SMEM((1,), I32),
            pltpu.SMEM((2,), I32),
            pltpu.SemaphoreType.DMA((5,)),
        ],
        flops=2 * SLOT_LANES * ROWS * PAIRS,
        moved=2 * PAIRS * ROWS * 3,
        out_specs=[VMEM] * 8 + [SMEM] * 3,
    )(virtual, row_start, column_start, turn, pair_label, table, amplitudes)

    def contract(steps, shards, sums):
        held = [] if sums is None else [sums]
        return call(
            functools.partial(contract_kernel, steps),
            "contract_" + "_".join(map(str, steps)),
            [VMEM] * (7 + len(shards)) + [ANY] * len(held),
            [shape((32, OUT_PAD, SLOT_LANES), jnp.int16)],
            [
                pltpu.VMEM((8 * len(steps), OUT_PAD, SLOT_LANES), jnp.int16),
                pltpu.VMEM((8 * OUT_PAD, SLOT_LANES), F32),
                pltpu.SemaphoreType.DMA((len(steps),)),
            ],
            flops=2 * 640 * len(steps) * PAIRS_PAD * 256,
            moved=2 * len(shards) * PACK * PAIRS_PAD,
            out_specs=ANY,
            aliases={} if sums is None else {7 + len(shards): 0},
        )(
            unpack,
            column_label,
            pair_label,
            rows_packed,
            more,
            rows_more,
            column_more,
            *shards,
            *held,
        )

    *found, own_more = call(
        place_kernel,
        "place",
        [SMEM] * 3 + [VMEM] * 3,
        [
            shape((SLOT_LANES, 896), BF16),
            shape((8, 896), F32),
            shape((OUT_PAD, 128), F32),
            shape((OUT_PAD, 128), F32),
        ],
    )(virtual, occupied, column_start, row_places, more, more_labels)
    from_1, from_3, rows_packed, *found = lax.optimization_barrier((from_1, from_3, rows_packed, *found))
    other_1, other_3 = to_sibling(from_1), to_sibling(from_3)
    sums = contract((0,), (packed, own_other), None)
    from_2, sums = lax.optimization_barrier((from_2, sums))
    other_2 = to_sibling(from_2)
    sums = contract((1, 3), (from_1, other_1, from_3, other_3), sums)
    sums = contract((2,), (from_2, other_2), sums)
    sums, *passes = lax.optimization_barrier((sums, *passes))
    parts = lax.all_to_all(sums, ("col", "depth"), 0, 0)
    return call(
        spread_kernel,
        "spread",
        [VMEM] * 8,
        [shape((OUT, ROWS), BF16)],
        [pltpu.VMEM((OUT_PAD, 896), F32)],
        flops=2 * OUT * ROWS * 128,
        moved=2 * 32 * OUT_PAD * SLOT_LANES,
    )(*found, own_more, row_places, more, parts, others(*passes))


def body(amplitudes, integrals, virtual_irrep, occupied_irrep, row_start, column_start):
    run = functools.partial(
        one_pass, amplitudes, integrals, virtual_irrep, occupied_irrep, row_start, column_start
    )
    def more(state):
        return state[0][0] > 0

    def again(state):
        left, out, spasses, wpasses = state
        turn = jnp.concatenate([lax.div(left, wpasses), lax.rem(left, wpasses)])
        return left - 1, run(turn, lambda *_: out), spasses, wpasses

    def other_passes(left, spasses, wpasses):
        nothing = jnp.zeros((OUT, ROWS), BF16)
        return lax.while_loop(more, again, (left, nothing, spasses, wpasses))[1]

    return run(jnp.zeros((2,), I32), other_passes)


def solution(mesh):
    return jax.shard_map(
        body,
        mesh=mesh,
        in_specs=(P("row", ("col", "depth")), P(("col", "depth"), "row"), P(), P(), P(), P()),
        out_specs=P(("col", "depth"), "row"),
        check_vma=False,
    )
```
